256 devices in a mesh: row: 32 (over z_lo, y, core), col: 8 (over z_hi, x).
Axes of the slice: x: 4, y: 4, z: 8 (z_hi: 2, z_lo: 4; z = z_hi * 4 + z_lo), core: 2. Of those that a mesh axis runs over, the one named last changes fastest.
Arguments:
- right_sides: bfloat16 [16384, 128, 128], P(('col', 'row')), may hold values from -6 to 6
- col_factors: bfloat16 [2, 16384, 128, 128], P(None, ('col', 'row')), may hold values from -0.5 to 0.5
- col_ranks: int32 [2, 16384], P(None, ('col', 'row')), may hold values from 64 to 128
- block_order: int32 [256, 64], P(('col', 'row')), may hold values from 0 to 63, each once within a row
- mid_factors: bfloat16 [8, 2048, 128, 128], P('col', 'row'), may hold values from -0.5 to 0.5
- mid_ranks: int32 [8, 2048], P('col', 'row'), may hold values from 64 to 128
- row_factors: bfloat16 [2048, 128, 128], P('row'), may hold values from -0.5 to 0.5
- row_ranks: int32 [2048], P('row'), may hold values from 64 to 128
Outputs:
- product: bfloat16 [2048, 128, 128], P(('row', 'col'))
The draws below stay inside these ranges and needn't reach their ends.
Inputs may be any that keep to these rules, and one draw needn't show every extreme that they name: Each row of block_order is a permutation of 0 to 63.
All inputs are finite; a program needn't handle non-finite values.
Results may differ from the reference program's by a relative error of at most 0.014.
Values may be sent and summed in bfloat16 or wider, within the bound.
No kernel may reach another device: no remote copies, remote signals or barrier semaphores. Data moves between devices by JAX's collectives and lax.ppermute only.
A program may use at most 64 MiB of HBM per device.

```python
import jax
import jax.numpy as jnp
from jax import lax

BW = 128
R = 128
PB = 64
GROUPS = 256
NB = 16384
NRB = 2048
Q = 2
N_ROW = 32
N_COL = 8


def set_ends(array, stream_key, least, largest):
    dims = array.shape
    place = [jax.random.randint(jax.random.fold_in(stream_key, axis), (), 0, dims[axis]) for axis in range(len(dims))]
    array = array.at[tuple(place)].set(least)
    longest = dims.index(max(dims))
    place[longest] = (place[longest] + 1) % dims[longest]
    return array.at[tuple(place)].set(largest)


def shard_levels(key, dims, pieces, smallest, top_value):
    def one(axis_at, shards_of):
        draws = jax.random.uniform(jax.random.fold_in(jax.random.fold_in(key, 6), axis_at), (shards_of,), jnp.float32, smallest / len(pieces), top_value / len(pieces))
        return jnp.repeat(jnp.exp(draws), dims[axis_at] // shards_of).reshape((-1,) + (1,) * (len(dims) - axis_at - 1))

    factor_of = one(*pieces[0])
    for cut in pieces[1:]:
        factor_of = factor_of * one(*cut)
    return factor_of


def normal_values(own_key, shape, deviation, reach, split=(), held_as=jnp.bfloat16):
    array = deviation * jax.random.normal(own_key, shape, jnp.float32)
    if split:
        array = array * shard_levels(own_key, shape, split, -0.22, 0.18)
    return jnp.clip(array, -reach, reach).astype(held_as)


def setup_inputs(seed: int = 0) -> dict:
    splits = jax.random.split(jax.random.key(seed), 9)
    right_sides = normal_values(splits[0], (NB, R, BW), 1.0, 6.0, ((0, 256),))
    col_factors = normal_values(splits[1], (2, NB, BW, BW), BW ** -0.5, 0.5, ((1, 256),))
    col_ranks = set_ends(jax.random.randint(splits[2], (2, NB), BW // 2, BW + 1), jax.random.fold_in(splits[2], 1), BW // 2, BW).astype(jnp.int32)
    block_order = jax.vmap(lambda own: jax.random.permutation(own, PB))(jax.random.split(splits[3], GROUPS)).reshape((GROUPS, PB)).astype(jnp.int32)
    mid_factors = normal_values(splits[4], (N_COL, NRB, BW, BW), BW ** -0.5, 0.5, ((0, 8), (1, 32)))
    mid_ranks = set_ends(jax.random.randint(splits[5], (N_COL, NRB), BW // 2, BW + 1), jax.random.fold_in(splits[5], 1), BW // 2, BW).astype(jnp.int32)
    row_factors = normal_values(splits[6], (NRB, BW, BW), BW ** -0.5, 0.5, ((0, 32),))
    row_ranks = set_ends(jax.random.randint(splits[7], (NRB,), BW // 2, BW + 1), jax.random.fold_in(splits[7], 1), BW // 2, BW).astype(jnp.int32)
    return dict(right_sides=right_sides, col_factors=col_factors, col_ranks=col_ranks, block_order=block_order, mid_factors=mid_factors, mid_ranks=mid_ranks, row_factors=row_factors, row_ranks=row_ranks)


def level(blocks, factors, ranks):
    keep = jnp.arange(BW)[None, :] < ranks[:, None]
    masked = jnp.where(keep[:, None, :], factors.astype(jnp.float32), jnp.float32(0))
    return jnp.einsum('nrk,nkj->nrj', blocks.astype(jnp.float32), masked)


def pair_halves(blocks):
    block_count = blocks.shape[0]
    side_count = blocks.shape[1]
    parts = blocks.reshape(block_count // 2, 2, side_count, 2, BW // 2)
    return parts.transpose(0, 3, 2, 1, 4).reshape(block_count, side_count, BW)


def reference(right_sides, col_factors, col_ranks, block_order, mid_factors, mid_ranks, row_factors, row_ranks):
    def column_group(group_id):
        offset = group_id * PB
        blocks = lax.dynamic_slice_in_dim(right_sides, offset, PB, 0)
        factors = lax.dynamic_slice_in_dim(col_factors, offset, PB, 1)
        ranks = lax.dynamic_slice_in_dim(col_ranks, offset, PB, 1)
        first = pair_halves(level(blocks, factors[0], ranks[0])).astype(jnp.bfloat16)
        middle = level(first, factors[1], ranks[1]).astype(jnp.bfloat16)
        return jnp.take(middle, block_order[group_id], axis=0)

    middles = lax.map(column_group, jnp.arange(N_COL * N_ROW, dtype=jnp.int32))
    regrouped = middles.reshape(N_COL, N_ROW, N_ROW, Q, R, BW).transpose(0, 2, 1, 3, 4, 5).reshape(N_COL, N_ROW, PB, R, BW)

    def row_group(row_id):
        offset = row_id * PB
        final_factors = lax.dynamic_slice_in_dim(row_factors, offset, PB, 0)
        final_ranks = lax.dynamic_slice_in_dim(row_ranks, offset, PB, 0)

        def add_group(total, col_id):
            blocks = regrouped[col_id, row_id]
            factors = lax.dynamic_slice_in_dim(mid_factors[col_id], offset, PB, 0)
            ranks = lax.dynamic_slice_in_dim(mid_ranks[col_id], offset, PB, 0)
            inner = pair_halves(level(blocks, factors, ranks)).astype(jnp.bfloat16)
            return total + level(inner, final_factors, final_ranks), None

        total, unused = lax.scan(add_group, jnp.zeros((PB, R, BW), jnp.float32), jnp.arange(N_COL, dtype=jnp.int32))
        return total.astype(jnp.bfloat16)

    outputs = lax.map(row_group, jnp.arange(N_ROW, dtype=jnp.int32))
    return outputs.reshape(N_ROW * PB, R, BW)
```

```python
import functools

import jax
import jax.numpy as jnp
from jax import lax
from jax.experimental import pallas as pl
from jax.experimental.pallas import tpu as pltpu
from jax.sharding import PartitionSpec as P

BW = 128
HALF = BW // 2
R = 128
PB = 64
STEP = 8
N_X = 4
N_Z = 2
OWN = 8
CHUNKS = (64, 64)


def masked_dot(blocks, factors, rank):
    product = jnp.dot(blocks, factors, preferred_element_type=jnp.float32)
    lane = lax.broadcasted_iota(jnp.int32, product.shape, 1)
    return jnp.where(lane < rank, product, 0.0)


def pair(even, odd):
    lane = lax.broadcasted_iota(jnp.int32, even.shape, 1)
    front = jnp.where(lane < HALF, even, pltpu.roll(odd, HALF, 1))
    back = jnp.where(lane < HALF, pltpu.roll(even, HALF, 1), odd)
    return front.astype(jnp.bfloat16), back.astype(jnp.bfloat16)


def col_kernel(start, rows, order_ref, rank_ref, z_ref, w_ref, out_ref, place_ref):
    step = pl.program_id(0)

    @pl.when(step == 0)
    def _():
        def put(k, carry):
            place_ref[order_ref[k]] = k
            return carry

        lax.fori_loop(0, PB, put, 0)

    for j in range(0, STEP, 2):
        b = step * STEP + j
        even = masked_dot(z_ref[j, start : start + rows], w_ref[0, j], rank_ref[0, b])
        odd = masked_dot(z_ref[j + 1, start : start + rows], w_ref[0, j + 1], rank_ref[0, b + 1])
        for i, block in enumerate(pair(even, odd)):
            middle = masked_dot(block, w_ref[1, j + i], rank_ref[1, b + i])
            out_ref[place_ref[b + i]] = middle.astype(jnp.bfloat16)


def col_levels(start, rows, order, ranks, right_sides, factors):
    return pl.pallas_call(
        functools.partial(col_kernel, start, rows),
        out_shape=jax.ShapeDtypeStruct((PB, rows, BW), jnp.bfloat16),
        grid_spec=pltpu.PrefetchScalarGridSpec(
            num_scalar_prefetch=2,
            grid=(PB // STEP,),
            in_specs=[
                pl.BlockSpec((STEP, R, BW), lambda g, *_: (g, 0, 0)),
                pl.BlockSpec((2, STEP, BW, BW), lambda g, *_: (0, g, 0, 0)),
            ],
            out_specs=pl.BlockSpec((PB, rows, BW), lambda g, *_: (0, 0, 0)),
            scratch_shapes=[pltpu.SMEM((PB,), jnp.int32)],
        ),
        cost_estimate=pl.CostEstimate(
            flops=4 * PB * rows * BW * BW, bytes_accessed=8 * 2**20, transcendentals=0
        ),
        name="col_levels",
    )(order, ranks, right_sides, factors)


def mid_kernel(x_ref, rank_ref, z_ref, w_ref, *out_refs):
    d, h = pl.program_id(0), pl.program_id(1)
    base = (h * N_X + lax.rem(x_ref[0] + d, N_X)) * STEP
    done = []
    for j in range(0, STEP, 2):
        even = masked_dot(z_ref[j], w_ref[j], rank_ref[base + j])
        odd = masked_dot(z_ref[j + 1], w_ref[j + 1], rank_ref[base + j + 1])
        done.extend(pair(even, odd))
    for k, out_ref in enumerate(out_refs):

        @pl.when(d == k)
        def _():
            for j, block in enumerate(done):
                out_ref[h * STEP + j] = block


def mid_level(rows, x, ranks, blocks, factors):
    def at(d, h, x_ref, rank_ref):
        return (h * N_X + lax.rem(x_ref[0] + d, N_X), 0, 0)

    piece = (N_Z * STEP, rows, BW)
    return pl.pallas_call(
        mid_kernel,
        out_shape=[jax.ShapeDtypeStruct(piece, jnp.bfloat16)] * N_X,
        grid_spec=pltpu.PrefetchScalarGridSpec(
            num_scalar_prefetch=2,
            grid=(N_X, N_Z),
            in_specs=[
                pl.BlockSpec((STEP, rows, BW), at),
                pl.BlockSpec((STEP, BW, BW), at),
            ],
            out_specs=[pl.BlockSpec(piece, lambda d, h, *_: (0, 0, 0))] * N_X,
        ),
        cost_estimate=pl.CostEstimate(
            flops=2 * PB * rows * BW * BW, bytes_accessed=6 * 2**20, transcendentals=0
        ),
        name="mid_level",
    )(x, ranks, blocks, factors)


def total_of(refs):
    total = refs[0][...].astype(jnp.float32)
    for ref in refs[1:]:
        total = total + ref[...].astype(jnp.float32)
    return total


def sum_kernel(z_ref, *refs):
    refs[-1][...] = total_of(refs[:-1]).astype(jnp.bfloat16)


def sum_other(rows, z, parts):
    return pl.pallas_call(
        sum_kernel,
        out_shape=jax.ShapeDtypeStruct((STEP, rows, BW), jnp.bfloat16),
        grid_spec=pltpu.PrefetchScalarGridSpec(
            num_scalar_prefetch=1,
            grid=(1,),
            in_specs=[pl.BlockSpec((STEP, rows, BW), lambda g, z_ref: (1 - z_ref[0], 0, 0))] * N_X,
            out_specs=pl.BlockSpec((STEP, rows, BW), lambda g, z_ref: (0, 0, 0)),
        ),
        cost_estimate=pl.CostEstimate(
            flops=4 * STEP * rows * BW, bytes_accessed=10 * STEP * rows * BW, transcendentals=0
        ),
        name="sum_other",
    )(z, *parts)


def row_kernel(chunks, me_ref, rank_ref, w_ref, *refs):
    out_ref = refs[-1]
    base = me_ref[0] * OWN
    start = 0
    for n, rows in enumerate(chunks):
        own = refs[n * (N_X + 1) : (n + 1) * (N_X + 1)]
        total = total_of(own).astype(jnp.bfloat16)
        for j in range(OWN):
            product = masked_dot(total[j], w_ref[j], rank_ref[base + j])
            out_ref[j, start : start + rows] = product.astype(jnp.bfloat16)
        start += rows


def row_level(chunks, me, ranks, factors, parts):
    in_specs = [pl.BlockSpec((OWN, BW, BW), lambda g, me_ref, *_: (me_ref[0], 0, 0))]
    for rows in chunks:
        half = pl.BlockSpec(
            (OWN, rows, BW), lambda g, me_ref, *_: (lax.div(me_ref[0], N_X), 0, 0)
        )
        in_specs += [half] * N_X + [pl.BlockSpec((OWN, rows, BW), lambda g, *_: (0, 0, 0))]
    return pl.pallas_call(
        functools.partial(row_kernel, chunks),
        out_shape=jax.ShapeDtypeStruct((OWN, R, BW), jnp.bfloat16),
        grid_spec=pltpu.PrefetchScalarGridSpec(
            num_scalar_prefetch=2,
            grid=(1,),
            in_specs=in_specs,
            out_specs=pl.BlockSpec((OWN, R, BW), lambda g, *_: (0, 0, 0)),
        ),
        cost_estimate=pl.CostEstimate(
            flops=2 * OWN * R * BW * BW, bytes_accessed=2**20, transcendentals=0
        ),
        name="row_level",
    )(me, ranks, factors, *parts)


def around_x(value, d):
    pairs = [(z * N_X + x, z * N_X + (x + d) % N_X) for z in range(N_Z) for x in range(N_X)]
    return lax.ppermute(value, "col", pairs)


def across_z(value):
    half = N_X * N_Z // 2
    return lax.ppermute(value, "col", [(i, (i + half) % (2 * half)) for i in range(2 * half)])


def shards(
    right_sides, col_factors, col_ranks, block_order, mid_factors, mid_ranks, row_factors, row_ranks
):
    me = lax.axis_index("col").astype(jnp.int32)
    x = lax.rem(me, N_X).reshape(1)
    z = lax.div(me, N_X).reshape(1)
    start = 0
    middles = []
    for rows in CHUNKS:
        middles.append(
            col_levels(start, rows, block_order[0], col_ranks, right_sides, col_factors)
        )
        start += rows
    parts = []
    for rows, middle in zip(CHUNKS, middles):
        regrouped = lax.all_to_all(middle, "row", split_axis=0, concat_axis=0, tiled=True)
        inner = mid_level(rows, x, mid_ranks[0], regrouped, mid_factors[0])
        near = [inner[0]] + [around_x(inner[d], d) for d in range(1, N_X)]
        far = across_z(sum_other(rows, z, near))
        parts += near + [far]
    return row_level(CHUNKS, me.reshape(1), row_ranks, row_factors, parts)


def solution(mesh):
    in_specs = (
        P(("col", "row"), None, None),
        P(None, ("col", "row"), None, None),
        P(None, ("col", "row")),
        P(("col", "row"), None),
        P("col", "row", None, None),
        P("col", "row"),
        P("row", None, None),
        P("row"),
    )
    out_specs = P(("row", "col"), None, None)
    return jax.shard_map(shards, mesh=mesh, in_specs=in_specs, out_specs=out_specs, check_vma=False)
```

```python
import functools

import jax
import jax.numpy as jnp
from jax import lax
from jax.experimental import pallas as pl
from jax.experimental.pallas import tpu as pltpu
from jax.sharding import PartitionSpec as P

BW = 128
HALF = BW // 2
R = 128
PB = 64
STEP = 8
N_X = 4
N_Z = 2
OWN = 8
CHUNKS = (64, 64)
BF16 = jnp.bfloat16
ANY = pl.BlockSpec(memory_space=pl.ANY)
SMEM = pl.BlockSpec(memory_space=pltpu.SMEM)
VMEM = pl.BlockSpec(memory_space=pltpu.VMEM)
SMALL = pltpu.CompilerParams(vmem_limit_bytes=12 * 2**20)


def masked_dot(blocks, factors, rank):
    product = jnp.dot(blocks, factors, preferred_element_type=jnp.float32)
    lane = lax.broadcasted_iota(jnp.int32, product.shape, 1)
    return jnp.where(lane < rank, product, 0.0)


def pair(even, odd):
    lane = lax.broadcasted_iota(jnp.int32, even.shape, 1)
    front = jnp.where(lane < HALF, even, pltpu.roll(odd, HALF, 1))
    back = jnp.where(lane < HALF, pltpu.roll(even, HALF, 1), odd)
    return front.astype(BF16), back.astype(BF16)


def col_kernel(order_ref, rank_ref, z_ref, w_ref, *refs):
    n = len(CHUNKS)
    out_refs, (z_buf, w_buf, place_ref, sems) = refs[:n], refs[n:]
    copies = []
    for g in range(PB // STEP):
        part = pl.ds(g * STEP, STEP)
        copies.append(
            [
                pltpu.make_async_copy(z_ref.at[part], z_buf.at[part], sems.at[0, g]),
                pltpu.make_async_copy(w_ref.at[0, part], w_buf.at[0, part], sems.at[1, g]),
                pltpu.make_async_copy(w_ref.at[1, part], w_buf.at[1, part], sems.at[2, g]),
            ]
        )
        for copy in copies[-1]:
            copy.start()
    for k in range(PB):
        place_ref[order_ref[k]] = k
    for g in range(PB // STEP):
        for copy in copies[g]:
            copy.wait()
        blocks = range(g * STEP, (g + 1) * STEP)
        first = [masked_dot(z_buf[b], w_buf[0, b], rank_ref[0, b]) for b in blocks]
        paired = []
        for j in range(0, STEP, 2):
            paired.extend(pair(first[j], first[j + 1]))
        for b, block in zip(blocks, paired):
            middle = masked_dot(block, w_buf[1, b], rank_ref[1, b]).astype(BF16)
            start = 0
            for rows, out_ref in zip(CHUNKS, out_refs):
                out_ref[place_ref[b]] = middle[start : start + rows]
                start += rows


def col_levels(order, ranks, right_sides, factors):
    return pl.pallas_call(
        col_kernel,
        out_shape=[jax.ShapeDtypeStruct((PB, rows, BW), BF16) for rows in CHUNKS],
        in_specs=[SMEM, SMEM, ANY, ANY],
        out_specs=[VMEM] * len(CHUNKS),
        scratch_shapes=[
            pltpu.VMEM((PB, R, BW), BF16),
            pltpu.VMEM((2, PB, BW, BW), BF16),
            pltpu.SMEM((PB,), jnp.int32),
            pltpu.SemaphoreType.DMA((3, PB // STEP)),
        ],
        cost_estimate=pl.CostEstimate(
            flops=4 * PB * R * BW * BW, bytes_accessed=8 * 2**20, transcendentals=0
        ),
        name="col_levels",
    )(order, ranks, right_sides, factors)


def mid_kernel(offsets, x_ref, rank_ref, z_ref, w_ref, *out_refs):
    for d, out_ref in zip(offsets, out_refs):
        for h in range(N_Z):
            base = (h * N_X + lax.rem(x_ref[0] + d, N_X)) * STEP
            for j in range(STEP):
                inner = masked_dot(z_ref[base + j], w_ref[base + j], rank_ref[base + j])
                out_ref[h * STEP + j] = inner.astype(BF16)


def mid_level(rows, offsets, x, ranks, blocks, factors):
    n = len(offsets)
    count = n * N_Z * STEP
    return pl.pallas_call(
        functools.partial(mid_kernel, offsets),
        out_shape=[jax.ShapeDtypeStruct((N_Z * STEP, rows, BW), BF16)] * n,
        in_specs=[SMEM, SMEM, VMEM, VMEM],
        out_specs=[VMEM] * n,
        compiler_params=SMALL,
        cost_estimate=pl.CostEstimate(
            flops=2 * count * rows * BW * BW,
            bytes_accessed=count * (4 * rows + 2 * BW) * BW,
            transcendentals=0,
        ),
        name="mid_level",
    )(x, ranks, blocks, factors)


def total_of(refs, half):
    total = refs[0][half].astype(jnp.float32)
    for ref in refs[1:]:
        total = total + ref[half].astype(jnp.float32)
    return total


def sum_kernel(z_ref, *refs):
    half = pl.ds((1 - z_ref[0]) * STEP, STEP)
    refs[N_X][...] = total_of(refs[:N_X], half).astype(BF16)


def sum_other(rows, z, parts):
    return pl.pallas_call(
        sum_kernel,
        out_shape=jax.ShapeDtypeStruct((STEP, rows, BW), BF16),
        in_specs=[SMEM] + [VMEM] * N_X,
        out_specs=VMEM,
        compiler_params=SMALL,
        cost_estimate=pl.CostEstimate(
            flops=4 * STEP * rows * BW, bytes_accessed=10 * STEP * rows * BW, transcendentals=0
        ),
        name="sum_other",
    )(z, *parts)


def row_kernel(me_ref, rank_ref, w_ref, *refs):
    out_ref = refs[-1]
    base = me_ref[0] * OWN
    half = pl.ds(lax.div(me_ref[0], N_X) * STEP, STEP)
    start = 0
    for n, rows in enumerate(CHUNKS):
        near = refs[n * (N_X + 1) : n * (N_X + 1) + N_X]
        far = refs[n * (N_X + 1) + N_X]
        total = total_of(near, half) + far[...].astype(jnp.float32)
        for j in range(0, OWN, 2):
            for i, block in enumerate(pair(total[j], total[j + 1])):
                product = masked_dot(block, w_ref[base + j + i], rank_ref[base + j + i])
                out_ref[j + i, start : start + rows] = product.astype(BF16)
        start += rows


def row_level(me, ranks, factors, parts):
    return pl.pallas_call(
        row_kernel,
        out_shape=jax.ShapeDtypeStruct((OWN, R, BW), BF16),
        in_specs=[SMEM, SMEM, VMEM] + [VMEM] * len(parts),
        out_specs=VMEM,
        compiler_params=SMALL,
        cost_estimate=pl.CostEstimate(
            flops=2 * OWN * R * BW * BW, bytes_accessed=2**20, transcendentals=0
        ),
        name="row_level",
    )(me, ranks, factors, *parts)


def around_x(value, d):
    pairs = [(z * N_X + x, z * N_X + (x + d) % N_X) for z in range(N_Z) for x in range(N_X)]
    return lax.ppermute(value, "col", pairs)


def across_z(value):
    half = N_X * N_Z // 2
    return lax.ppermute(value, "col", [(i, (i + half) % (2 * half)) for i in range(2 * half)])


def shards(
    right_sides, col_factors, col_ranks, block_order, mid_factors, mid_ranks, row_factors, row_ranks
):
    me = lax.axis_index("col").astype(jnp.int32)
    x = lax.rem(me, N_X).reshape(1)
    z = lax.div(me, N_X).reshape(1)
    middles = col_levels(block_order[0], col_ranks, right_sides, col_factors)
    parts = []
    before = None
    for rows, middle in zip(CHUNKS, middles):
        regrouped = lax.all_to_all(middle, "row", split_axis=0, concat_axis=0, tiled=True)
        if before is not None:
            regrouped, before = lax.optimization_barrier((regrouped, before))
            parts.append(across_z(before))
        sent = mid_level(rows, (2, 1, 3), x, mid_ranks[0], regrouped, mid_factors[0])
        kept = mid_level(rows, (0,), x, mid_ranks[0], regrouped, mid_factors[0])
        near = list(kept) + [around_x(piece, d) for piece, d in zip(sent, (2, 1, 3))]
        before = sum_other(rows, z, near)
        parts += near
    parts.append(across_z(before))
    return row_level(me.reshape(1), row_ranks, row_factors, parts)


def solution(mesh):
    in_specs = (
        P(("col", "row"), None, None),
        P(None, ("col", "row"), None, None),
        P(None, ("col", "row")),
        P(("col", "row"), None),
        P("col", "row", None, None),
        P("col", "row"),
        P("row", None, None),
        P("row"),
    )
    out_specs = P(("row", "col"), None, None)
    return jax.shard_map(shards, mesh=mesh, in_specs=in_specs, out_specs=out_specs, check_vma=False)
```

```python
import functools

import jax
import jax.numpy as jnp
from jax import lax
from jax.experimental import pallas as pl
from jax.experimental.pallas import tpu as pltpu
from jax.sharding import PartitionSpec as P

BW = 128
HALF = BW // 2
R = 128
PB = 64
STEP = 8
N_X = 4
N_Z = 2
OWN = 8
N_PLANE = 4
N_Y = 4
N_CORE = 2
Q = 2
PIECE = 16
CHUNKS = (80, 48)
BF16 = jnp.bfloat16
ANY = pl.BlockSpec(memory_space=pl.ANY)
SMEM = pl.BlockSpec(memory_space=pltpu.SMEM)
VMEM = pl.BlockSpec(memory_space=pltpu.VMEM)
SMALL = pltpu.CompilerParams(vmem_limit_bytes=12 * 2**20)


def masked_dot(blocks, factors, rank):
    product = jnp.dot(blocks, factors, preferred_element_type=jnp.float32)
    lane = lax.broadcasted_iota(jnp.int32, product.shape, 1)
    return jnp.where(lane < rank, product, 0.0)


def pair(even, odd):
    lane = lax.broadcasted_iota(jnp.int32, even.shape, 1)
    front = jnp.where(lane < HALF, even, pltpu.roll(odd, HALF, 1))
    back = jnp.where(lane < HALF, pltpu.roll(even, HALF, 1), odd)
    return front.astype(BF16), back.astype(BF16)


def col_kernel(at_ref, order_ref, rank_ref, z_ref, w_ref, *refs):
    straight_ref, out_refs = refs[0], refs[1 : 1 + N_CORE]
    z_buf, w_buf, first_buf, sems = refs[1 + N_CORE :]
    early, late = [], []
    for g in range(PB // STEP):
        part = pl.ds(g * STEP, STEP)
        early.append(pltpu.make_async_copy(z_ref.at[part], z_buf.at[part], sems.at[0, g]))
        early.append(pltpu.make_async_copy(w_ref.at[0, part], w_buf.at[0, part], sems.at[1, g]))
        late.append(pltpu.make_async_copy(w_ref.at[1, part], w_buf.at[1, part], sems.at[2, g]))
    for copy in early + late:
        copy.start()
    for g in range(PB // STEP):
        early[2 * g].wait()
        early[2 * g + 1].wait()
        blocks = range(g * STEP, (g + 1) * STEP)
        first = [masked_dot(z_buf[b], w_buf[0, b], rank_ref[0, b]) for b in blocks]
        for j in range(0, STEP, 2):
            front, back = pair(first[j], first[j + 1])
            first_buf[g * STEP + j] = front
            first_buf[g * STEP + j + 1] = back
    for copy in late:
        copy.wait()
    rows = CHUNKS[0]
    for e in range(N_CORE):
        for k in range(N_PLANE):
            for m in range(N_Y):
                for i in range(Q):
                    place = (at_ref[0] ^ flip(k, m, e)) * Q + i
                    b = order_ref[place]
                    middle = masked_dot(first_buf[b], w_buf[1, b], rank_ref[1, b]).astype(BF16)
                    straight_ref[place] = middle[:rows]
                    out_refs[e][(k * N_Y + m) * Q + i] = middle[rows:]


def flip(k, m, e):
    return (k * N_Y + m) * N_CORE + e


def col_levels(at, order, ranks, right_sides, factors):
    straight, stepped = CHUNKS
    return pl.pallas_call(
        col_kernel,
        out_shape=[jax.ShapeDtypeStruct((PB, straight, BW), BF16)]
        + [jax.ShapeDtypeStruct((PB // N_CORE, stepped, BW), BF16)] * N_CORE,
        in_specs=[SMEM, SMEM, SMEM, ANY, ANY],
        out_specs=[VMEM] * (1 + N_CORE),
        scratch_shapes=[
            pltpu.VMEM((PB, R, BW), BF16),
            pltpu.VMEM((2, PB, BW, BW), BF16),
            pltpu.VMEM((PB, R, BW), BF16),
            pltpu.SemaphoreType.DMA((3, PB // STEP)),
        ],
        cost_estimate=pl.CostEstimate(
            flops=4 * PB * R * BW * BW, bytes_accessed=8 * 2**20, transcendentals=0
        ),
        name="col_levels",
    )(at, order, ranks, right_sides, factors)


def regroup_kernel(moves, n_in, *refs):
    for source, start, target, place in moves:
        refs[n_in + target][place : place + Q] = refs[source][start : start + Q]


def regroup(rows, moves, n_out, pieces):
    return pl.pallas_call(
        functools.partial(regroup_kernel, moves, len(pieces)),
        out_shape=[jax.ShapeDtypeStruct((PIECE, rows, BW), BF16)] * n_out,
        in_specs=[VMEM] * len(pieces),
        out_specs=[VMEM] * n_out,
        compiler_params=SMALL,
        cost_estimate=pl.CostEstimate(
            flops=0, bytes_accessed=4 * n_out * PIECE * rows * BW, transcendentals=0
        ),
        name="regroup",
    )(*pieces)


def for_y():
    moves = []
    for m in range(1, N_Y):
        for e in range(N_CORE):
            for k in range(N_PLANE):
                moves.append((e, (k * N_Y + m) * Q, m - 1, (e * N_PLANE + k) * Q))
    return moves


def for_planes():
    moves = []
    for k in range(N_PLANE):
        for m in range(N_Y):
            for e in range(N_CORE):
                place = (m * N_CORE + e) * Q
                if m == 0:
                    moves.append((e, k * N_Y * Q, k, place))
                else:
                    moves.append((N_CORE + m - 1, (e * N_PLANE + k) * Q, k, place))
    return moves


def mid_kernel(offsets, at_ref, rank_ref, z_ref, w_ref, *out_refs):
    for d, out_ref in zip(offsets, out_refs):
        for h in range(N_Z):
            base = (h * N_X + lax.rem(at_ref[1] + d, N_X)) * STEP
            for j in range(STEP):
                inner = masked_dot(z_ref[base + j], w_ref[base + j], rank_ref[base + j])
                out_ref[h * STEP + j] = inner.astype(BF16)


def mid_level(rows, offsets, at, ranks, blocks, factors):
    n = len(offsets)
    count = n * N_Z * STEP
    return pl.pallas_call(
        functools.partial(mid_kernel, offsets),
        out_shape=[jax.ShapeDtypeStruct((N_Z * STEP, rows, BW), BF16)] * n,
        in_specs=[SMEM, SMEM, VMEM, VMEM],
        out_specs=[VMEM] * n,
        compiler_params=SMALL,
        cost_estimate=pl.CostEstimate(
            flops=2 * count * rows * BW * BW,
            bytes_accessed=count * (4 * rows + 2 * BW) * BW,
            transcendentals=0,
        ),
        name="mid_level",
    )(at, ranks, blocks, factors)


def stepped_kernel(at_ref, rank_ref, w_ref, *refs):
    pieces, out_refs, inner_buf = refs[:N_PLANE], refs[N_PLANE:-1], refs[-1]
    for k in range(N_PLANE):
        for m in range(N_Y):
            for e in range(N_CORE):
                for i in range(Q):
                    b = (at_ref[0] ^ flip(k, m, e)) * Q + i
                    block = pieces[k][(m * N_CORE + e) * Q + i]
                    inner_buf[b] = masked_dot(block, w_ref[b], rank_ref[b]).astype(BF16)
    for d, out_ref in enumerate(out_refs):
        for h in range(N_Z):
            base = (h * N_X + lax.rem(at_ref[1] + d, N_X)) * STEP
            out_ref[h * STEP : (h + 1) * STEP] = inner_buf[pl.ds(base, STEP)]


def mid_stepped(rows, at, ranks, factors, pieces):
    return pl.pallas_call(
        stepped_kernel,
        out_shape=[jax.ShapeDtypeStruct((N_Z * STEP, rows, BW), BF16)] * N_X,
        in_specs=[SMEM, SMEM, VMEM] + [VMEM] * N_PLANE,
        out_specs=[VMEM] * N_X,
        scratch_shapes=[pltpu.VMEM((PB, rows, BW), BF16)],
        compiler_params=SMALL,
        cost_estimate=pl.CostEstimate(
            flops=2 * PB * rows * BW * BW,
            bytes_accessed=PB * (4 * rows + 2 * BW) * BW,
            transcendentals=0,
        ),
        name="mid_stepped",
    )(at, ranks, factors, *pieces)


def total_of(refs, half):
    total = refs[0][half].astype(jnp.float32)
    for ref in refs[1:]:
        total = total + ref[half].astype(jnp.float32)
    return total


def sum_kernel(at_ref, *refs):
    half = pl.ds((1 - at_ref[2]) * STEP, STEP)
    refs[N_X][...] = total_of(refs[:N_X], half).astype(BF16)


def sum_other(rows, at, parts):
    return pl.pallas_call(
        sum_kernel,
        out_shape=jax.ShapeDtypeStruct((STEP, rows, BW), BF16),
        in_specs=[SMEM] + [VMEM] * N_X,
        out_specs=VMEM,
        compiler_params=SMALL,
        cost_estimate=pl.CostEstimate(
            flops=4 * STEP * rows * BW, bytes_accessed=10 * STEP * rows * BW, transcendentals=0
        ),
        name="sum_other",
    )(at, *parts)


def row_kernel(at_ref, rank_ref, w_ref, *refs):
    out_ref = refs[-1]
    base = at_ref[3] * OWN
    half = pl.ds(at_ref[2] * STEP, STEP)
    start = 0
    for n, rows in enumerate(CHUNKS):
        near = refs[n * (N_X + 1) : n * (N_X + 1) + N_X]
        far = refs[n * (N_X + 1) + N_X]
        total = total_of(near, half) + far[...].astype(jnp.float32)
        for j in range(0, OWN, 2):
            for i, block in enumerate(pair(total[j], total[j + 1])):
                product = masked_dot(block, w_ref[base + j + i], rank_ref[base + j + i])
                out_ref[j + i, start : start + rows] = product.astype(BF16)
        start += rows


def row_level(at, ranks, factors, parts):
    return pl.pallas_call(
        row_kernel,
        out_shape=jax.ShapeDtypeStruct((OWN, R, BW), BF16),
        in_specs=[SMEM, SMEM, VMEM] + [VMEM] * len(parts),
        out_specs=VMEM,
        compiler_params=SMALL,
        cost_estimate=pl.CostEstimate(
            flops=2 * OWN * R * BW * BW, bytes_accessed=2**20, transcendentals=0
        ),
        name="row_level",
    )(at, ranks, factors, *parts)


def around_x(value, d):
    pairs = [(z * N_X + x, z * N_X + (x + d) % N_X) for z in range(N_Z) for x in range(N_X)]
    return lax.ppermute(value, "col", pairs)


def across_z(value):
    half = N_X * N_Z // 2
    return lax.ppermute(value, "col", [(i, (i + half) % (2 * half)) for i in range(2 * half)])


def across_row(value, k, m, e):
    return lax.ppermute(
        value, "row", [(r, r ^ flip(k, m, e)) for r in range(N_PLANE * N_Y * N_CORE)]
    )


def shards(
    right_sides, col_factors, col_ranks, block_order, mid_factors, mid_ranks, row_factors, row_ranks
):
    me = lax.axis_index("col").astype(jnp.int32)
    row = lax.axis_index("row").astype(jnp.int32)
    at = jnp.stack([row, lax.rem(me, N_X), lax.div(me, N_X), me])
    ranks, factors = mid_ranks[0], mid_factors[0]
    straight_rows, stepped_rows = CHUNKS
    middle, same, other = col_levels(at, block_order[0], col_ranks, right_sides, col_factors)

    regrouped = lax.all_to_all(middle, "row", split_axis=0, concat_axis=0, tiled=True)

    cores = [same, across_row(other, 0, 0, 1)]
    pieces = regroup(stepped_rows, for_y(), N_Y - 1, cores)
    lines = [across_row(piece, 0, m + 1, 0) for m, piece in enumerate(pieces)]
    pieces = regroup(stepped_rows, for_planes(), N_PLANE, cores + lines)
    planes = [pieces[0]] + [across_row(pieces[k], k, 0, 0) for k in range(1, N_PLANE)]

    sent = mid_level(straight_rows, (2, 1, 3), at, ranks, regrouped, factors)
    kept = mid_level(straight_rows, (0,), at, ranks, regrouped, factors)
    near = list(kept) + [around_x(piece, d) for piece, d in zip(sent, (2, 1, 3))]
    parts = near + [across_z(sum_other(straight_rows, at, near))]

    inner = mid_stepped(stepped_rows, at, ranks, factors, planes)
    near = [inner[0]] + [around_x(inner[d], d) for d in (2, 1, 3)]
    parts += near + [across_z(sum_other(stepped_rows, at, near))]
    return row_level(at, row_ranks, row_factors, parts)


def solution(mesh):
    in_specs = (
        P(("col", "row"), None, None),
        P(None, ("col", "row"), None, None),
        P(None, ("col", "row")),
        P(("col", "row"), None),
        P("col", "row", None, None),
        P("col", "row"),
        P("row", None, None),
        P("row"),
    )
    out_specs = P(("row", "col"), None, None)
    return jax.shard_map(shards, mesh=mesh, in_specs=in_specs, out_specs=out_specs, check_vma=False)
```

```python
import functools

import jax
import jax.numpy as jnp
from jax import lax
from jax.experimental import pallas as pl
from jax.experimental.pallas import tpu as pltpu
from jax.sharding import PartitionSpec as P

BW = 128
HALF = BW // 2
R = 128
PB = 64
STEP = 8
N_X = 4
N_Z = 2
OWN = 8
N_PLANE = 4
N_Y = 4
N_CORE = 2
Q = 2
PIECE = 16
CHUNKS = (80, 48)
BF16 = jnp.bfloat16
ANY = pl.BlockSpec(memory_space=pl.ANY)
SMEM = pl.BlockSpec(memory_space=pltpu.SMEM)
VMEM = pl.BlockSpec(memory_space=pltpu.VMEM)
SMALL = pltpu.CompilerParams(vmem_limit_bytes=12 * 2**20)


def masked_dot(blocks, factors, rank):
    product = jnp.dot(blocks, factors, preferred_element_type=jnp.float32)
    lane = lax.broadcasted_iota(jnp.int32, product.shape, 1)
    return jnp.where(lane < rank, product, 0.0)


def pair(even, odd):
    lane = lax.broadcasted_iota(jnp.int32, even.shape, 1)
    front = jnp.where(lane < HALF, even, pltpu.roll(odd, HALF, 1))
    back = jnp.where(lane < HALF, pltpu.roll(even, HALF, 1), odd)
    return front.astype(BF16), back.astype(BF16)


def col_kernel(row_ref, me_ref, order_ref, rank_ref, z_ref, w_ref, *refs):
    straight_ref, out_refs = refs[0], refs[1 : 1 + N_CORE]
    z_buf, w_buf, first_buf, sems = refs[1 + N_CORE :]
    early, late = [], []
    for g in range(PB // STEP):
        part = pl.ds(g * STEP, STEP)
        early.append(pltpu.make_async_copy(z_ref.at[part], z_buf.at[part], sems.at[0, g]))
        early.append(pltpu.make_async_copy(w_ref.at[0, part], w_buf.at[0, part], sems.at[1, g]))
        late.append(pltpu.make_async_copy(w_ref.at[1, part], w_buf.at[1, part], sems.at[2, g]))
    for copy in early + late:
        copy.start()
    for g in range(PB // STEP):
        early[2 * g].wait()
        early[2 * g + 1].wait()
        blocks = range(g * STEP, (g + 1) * STEP)
        first = [masked_dot(z_buf[b], w_buf[0, b], rank_ref[0, b]) for b in blocks]
        for j in range(0, STEP, 2):
            front, back = pair(first[j], first[j + 1])
            first_buf[g * STEP + j] = front
            first_buf[g * STEP + j + 1] = back
    for copy in late:
        copy.wait()
    rows = CHUNKS[0]
    for e in range(N_CORE):
        for k in range(N_PLANE):
            for m in range(N_Y):
                for i in range(Q):
                    place = (row_ref[0] ^ flip(k, m, e)) * Q + i
                    b = order_ref[place]
                    middle = masked_dot(first_buf[b], w_buf[1, b], rank_ref[1, b]).astype(BF16)
                    straight_ref[place] = middle[:rows]
                    out_refs[e][(k * N_Y + m) * Q + i] = middle[rows:]


def flip(k, m, e):
    return (k * N_Y + m) * N_CORE + e


def col_levels(row, me, order, ranks, right_sides, factors):
    straight, stepped = CHUNKS
    return pl.pallas_call(
        col_kernel,
        out_shape=[jax.ShapeDtypeStruct((PB, straight, BW), BF16)]
        + [jax.ShapeDtypeStruct((PB // N_CORE, stepped, BW), BF16)] * N_CORE,
        in_specs=[SMEM, SMEM, SMEM, SMEM, ANY, ANY],
        out_specs=[VMEM] * (1 + N_CORE),
        scratch_shapes=[
            pltpu.VMEM((PB, R, BW), BF16),
            pltpu.VMEM((2, PB, BW, BW), BF16),
            pltpu.VMEM((PB, R, BW), BF16),
            pltpu.SemaphoreType.DMA((3, PB // STEP)),
        ],
        cost_estimate=pl.CostEstimate(
            flops=4 * PB * R * BW * BW, bytes_accessed=8 * 2**20, transcendentals=0
        ),
        name="col_levels",
    )(row, me, order, ranks, right_sides, factors)


def regroup_kernel(moves, n_in, *refs):
    for source, start, target, place in moves:
        refs[n_in + target][place : place + Q] = refs[source][start : start + Q]


def regroup(rows, moves, n_out, pieces):
    return pl.pallas_call(
        functools.partial(regroup_kernel, moves, len(pieces)),
        out_shape=[jax.ShapeDtypeStruct((PIECE, rows, BW), BF16)] * n_out,
        in_specs=[VMEM] * len(pieces),
        out_specs=[VMEM] * n_out,
        compiler_params=SMALL,
        cost_estimate=pl.CostEstimate(
            flops=0, bytes_accessed=4 * n_out * PIECE * rows * BW, transcendentals=0
        ),
        name="regroup",
    )(*pieces)


def for_y():
    moves = []
    for m in range(1, N_Y):
        for e in range(N_CORE):
            for k in range(N_PLANE):
                moves.append((e, (k * N_Y + m) * Q, m - 1, (e * N_PLANE + k) * Q))
    return moves


def for_planes():
    moves = []
    for k in range(N_PLANE):
        for m in range(N_Y):
            for e in range(N_CORE):
                place = (m * N_CORE + e) * Q
                if m == 0:
                    moves.append((e, k * N_Y * Q, k, place))
                else:
                    moves.append((N_CORE + m - 1, (e * N_PLANE + k) * Q, k, place))
    return moves


def mid_kernel(offsets, me_ref, rank_ref, z_ref, w_ref, *out_refs):
    for d, out_ref in zip(offsets, out_refs):
        for h in range(N_Z):
            base = (h * N_X + lax.rem(me_ref[0] + d, N_X)) * STEP
            for j in range(STEP):
                inner = masked_dot(z_ref[base + j], w_ref[base + j], rank_ref[base + j])
                out_ref[h * STEP + j] = inner.astype(BF16)


def mid_level(rows, offsets, me, ranks, blocks, factors):
    n = len(offsets)
    count = n * N_Z * STEP
    return pl.pallas_call(
        functools.partial(mid_kernel, offsets),
        out_shape=[jax.ShapeDtypeStruct((N_Z * STEP, rows, BW), BF16)] * n,
        in_specs=[SMEM, SMEM, VMEM, VMEM],
        out_specs=[VMEM] * n,
        compiler_params=SMALL,
        cost_estimate=pl.CostEstimate(
            flops=2 * count * rows * BW * BW,
            bytes_accessed=count * (4 * rows + 2 * BW) * BW,
            transcendentals=0,
        ),
        name="mid_level",
    )(me, ranks, blocks, factors)


def stepped_kernel(row_ref, me_ref, rank_ref, w_ref, *refs):
    pieces, out_refs, inner_buf = refs[:N_PLANE], refs[N_PLANE:-1], refs[-1]
    for k in range(N_PLANE):
        for m in range(N_Y):
            for e in range(N_CORE):
                for i in range(Q):
                    b = (row_ref[0] ^ flip(k, m, e)) * Q + i
                    block = pieces[k][(m * N_CORE + e) * Q + i]
                    inner_buf[b] = masked_dot(block, w_ref[b], rank_ref[b]).astype(BF16)
    for d, out_ref in enumerate(out_refs):
        for h in range(N_Z):
            base = (h * N_X + lax.rem(me_ref[0] + d, N_X)) * STEP
            out_ref[h * STEP : (h + 1) * STEP] = inner_buf[pl.ds(base, STEP)]


def mid_stepped(rows, row, me, ranks, factors, pieces):
    return pl.pallas_call(
        stepped_kernel,
        out_shape=[jax.ShapeDtypeStruct((N_Z * STEP, rows, BW), BF16)] * N_X,
        in_specs=[SMEM, SMEM, SMEM, VMEM] + [VMEM] * N_PLANE,
        out_specs=[VMEM] * N_X,
        scratch_shapes=[pltpu.VMEM((PB, rows, BW), BF16)],
        compiler_params=SMALL,
        cost_estimate=pl.CostEstimate(
            flops=2 * PB * rows * BW * BW,
            bytes_accessed=PB * (4 * rows + 2 * BW) * BW,
            transcendentals=0,
        ),
        name="mid_stepped",
    )(row, me, ranks, factors, *pieces)


def total_of(refs, half):
    total = refs[0][half].astype(jnp.float32)
    for ref in refs[1:]:
        total = total + ref[half].astype(jnp.float32)
    return total


def sum_kernel(me_ref, *refs):
    half = pl.ds((1 - lax.div(me_ref[0], N_X)) * STEP, STEP)
    refs[N_X][...] = total_of(refs[:N_X], half).astype(BF16)


def sum_other(rows, me, parts):
    return pl.pallas_call(
        sum_kernel,
        out_shape=jax.ShapeDtypeStruct((STEP, rows, BW), BF16),
        in_specs=[SMEM] + [VMEM] * N_X,
        out_specs=VMEM,
        compiler_params=SMALL,
        cost_estimate=pl.CostEstimate(
            flops=4 * STEP * rows * BW, bytes_accessed=10 * STEP * rows * BW, transcendentals=0
        ),
        name="sum_other",
    )(me, *parts)


def row_kernel(me_ref, rank_ref, w_ref, *refs):
    out_ref = refs[-1]
    base = me_ref[0] * OWN
    half = pl.ds(lax.div(me_ref[0], N_X) * STEP, STEP)
    start = 0
    for n, rows in enumerate(CHUNKS):
        near = refs[n * (N_X + 1) : n * (N_X + 1) + N_X]
        far = refs[n * (N_X + 1) + N_X]
        total = total_of(near, half) + far[...].astype(jnp.float32)
        for j in range(0, OWN, 2):
            for i, block in enumerate(pair(total[j], total[j + 1])):
                product = masked_dot(block, w_ref[base + j + i], rank_ref[base + j + i])
                out_ref[j + i, start : start + rows] = product.astype(BF16)
        start += rows


def row_level(me, ranks, factors, parts):
    return pl.pallas_call(
        row_kernel,
        out_shape=jax.ShapeDtypeStruct((OWN, R, BW), BF16),
        in_specs=[SMEM, SMEM, VMEM] + [VMEM] * len(parts),
        out_specs=VMEM,
        compiler_params=SMALL,
        cost_estimate=pl.CostEstimate(
            flops=2 * OWN * R * BW * BW, bytes_accessed=2**20, transcendentals=0
        ),
        name="row_level",
    )(me, ranks, factors, *parts)


def around_x(value, d):
    pairs = [(z * N_X + x, z * N_X + (x + d) % N_X) for z in range(N_Z) for x in range(N_X)]
    return lax.ppermute(value, "col", pairs)


def across_z(value):
    half = N_X * N_Z // 2
    return lax.ppermute(value, "col", [(i, (i + half) % (2 * half)) for i in range(2 * half)])


def across_row(value, k, m, e):
    return lax.ppermute(
        value, "row", [(r, r ^ flip(k, m, e)) for r in range(N_PLANE * N_Y * N_CORE)]
    )


def shards(
    right_sides, col_factors, col_ranks, block_order, mid_factors, mid_ranks, row_factors, row_ranks
):
    me = lax.axis_index("col").astype(jnp.int32).reshape(1)
    row = lax.axis_index("row").astype(jnp.int32).reshape(1)
    ranks, factors = mid_ranks[0], mid_factors[0]
    straight_rows, stepped_rows = CHUNKS
    middle, same, other = col_levels(
        row, me, block_order[0], col_ranks, right_sides, col_factors
    )

    regrouped = lax.all_to_all(middle, "row", split_axis=0, concat_axis=0, tiled=True)

    cores = [same, across_row(other, 0, 0, 1)]
    pieces = regroup(stepped_rows, for_y(), N_Y - 1, cores)
    lines = [across_row(piece, 0, m + 1, 0) for m, piece in enumerate(pieces)]
    pieces = regroup(stepped_rows, for_planes(), N_PLANE, cores + lines)
    planes = [pieces[0]] + [across_row(pieces[k], k, 0, 0) for k in range(1, N_PLANE)]

    inner = mid_level(straight_rows, (0, 1, 2, 3), me, ranks, regrouped, factors)
    near = [inner[0]] + [around_x(inner[d], d) for d in (2, 1, 3)]
    parts = near + [across_z(sum_other(straight_rows, me, near))]

    inner = mid_stepped(stepped_rows, row, me, ranks, factors, planes)
    near = [inner[0]] + [around_x(inner[d], d) for d in (2, 1, 3)]
    parts += near + [across_z(sum_other(stepped_rows, me, near))]
    return row_level(me, row_ranks, row_factors, parts)


def solution(mesh):
    in_specs = (
        P(("col", "row"), None, None),
        P(None, ("col", "row"), None, None),
        P(None, ("col", "row")),
        P(("col", "row"), None),
        P("col", "row", None, None),
        P("col", "row"),
        P("row", None, None),
        P("row"),
    )
    out_specs = P(("row", "col"), None, None)
    return jax.shard_map(shards, mesh=mesh, in_specs=in_specs, out_specs=out_specs, check_vma=False)
```

```python
import functools

import jax
import jax.numpy as jnp
from jax import lax
from jax.experimental import pallas as pl
from jax.experimental.pallas import tpu as pltpu
from jax.sharding import PartitionSpec as P

BW = 128
HALF = BW // 2
R = 128
PB = 64
STEP = 8
N_X = 4
N_Z = 2
OWN = 8
N_PLANE = 4
N_Y = 4
N_CORE = 2
PLANE = N_Y * N_CORE
Q = 2
PIECE = 16
EARLY = 3
HINT_CORE = 100000000000
HINT_Y = 0
HINT_PLANES = 0
HINT_MID = 100000000000
HINT_STEPPED = 100000000000
CHUNKS = (80, 48)
BF16 = jnp.bfloat16
ANY = pl.BlockSpec(memory_space=pl.ANY)
SMEM = pl.BlockSpec(memory_space=pltpu.SMEM)
VMEM = pl.BlockSpec(memory_space=pltpu.VMEM)
SMALL = pltpu.CompilerParams(vmem_limit_bytes=12 * 2**20)


def masked_dot(blocks, factors, rank):
    product = jnp.dot(blocks, factors, preferred_element_type=jnp.float32)
    lane = lax.broadcasted_iota(jnp.int32, product.shape, 1)
    return jnp.where(lane < rank, product, 0.0)


def pair(even, odd):
    lane = lax.broadcasted_iota(jnp.int32, even.shape, 1)
    front = jnp.where(lane < HALF, even, pltpu.roll(odd, HALF, 1))
    back = jnp.where(lane < HALF, pltpu.roll(even, HALF, 1), odd)
    return front.astype(BF16), back.astype(BF16)


def col_kernel(row_ref, me_ref, order_ref, rank_ref, z_ref, w_ref, *refs):
    out_refs, (z_buf, w_buf, first_buf, sems) = refs[: 2 + N_CORE], refs[2 + N_CORE : 6 + N_CORE]
    straight_buf, early_buf, *bufs = refs[6 + N_CORE : -1]
    out_sems = refs[-1]
    early, late = [], []
    for g in range(PB // STEP):
        part = pl.ds(g * STEP, STEP)
        early.append(pltpu.make_async_copy(z_ref.at[part], z_buf.at[part], sems.at[0, g]))
        early.append(pltpu.make_async_copy(w_ref.at[0, part], w_buf.at[0, part], sems.at[1, g]))
        late.append(pltpu.make_async_copy(w_ref.at[1, part], w_buf.at[1, part], sems.at[2, g]))
    for copy in early + late:
        copy.start()
    for g in range(PB // STEP):
        early[2 * g].wait()
        early[2 * g + 1].wait()
        blocks = range(g * STEP, (g + 1) * STEP)
        first = [masked_dot(z_buf[b], w_buf[0, b], rank_ref[0, b]) for b in blocks]
        for j in range(0, STEP, 2):
            front, back = pair(first[j], first[j + 1])
            first_buf[g * STEP + j] = front
            first_buf[g * STEP + j + 1] = back
    for copy in late:
        copy.wait()
    rows = CHUNKS[0]
    outs = []

    def send(buf, place, out_ref, start, count):
        copy = pltpu.make_async_copy(
            buf.at[pl.ds(place, count)], out_ref.at[pl.ds(start, count)], out_sems.at[len(outs)]
        )
        copy.start()
        outs.append(copy)

    for k in reversed(range(N_PLANE)):
        for m in range(N_Y):
            for e in range(N_CORE):
                for i in range(Q):
                    n = (m * N_CORE + e) * Q + i
                    place = (row_ref[0] ^ flip(k, m, e)) * Q + i
                    b = order_ref[place]
                    middle = masked_dot(first_buf[b], w_buf[1, b], rank_ref[1, b]).astype(BF16)
                    straight_buf[k * PIECE + near_place(row_ref, m, e) + i] = middle[:rows]
                    if k == EARLY:
                        early_buf[n] = middle[rows:]
                    else:
                        bufs[e][(k * N_Y + m) * Q + i] = middle[rows:]
        start = ((row_ref[0] // PLANE) ^ k) * PIECE
        send(straight_buf, k * PIECE, out_refs[0], start, PIECE)
        if k == EARLY:
            send(early_buf, 0, out_refs[1], 0, PIECE)
        else:
            for e in range(N_CORE):
                send(bufs[e], k * N_Y * Q, out_refs[2 + e], k * N_Y * Q, N_Y * Q)
    for copy in outs:
        copy.wait()


def near_place(row_ref, m, e):
    return ((row_ref[0] % PLANE) ^ (m * N_CORE + e)) * Q


def flip(k, m, e):
    return (k * N_Y + m) * N_CORE + e


def col_levels(row, me, order, ranks, right_sides, factors):
    straight, stepped = CHUNKS
    return pl.pallas_call(
        col_kernel,
        out_shape=[jax.ShapeDtypeStruct((PB, straight, BW), BF16)]
        + [jax.ShapeDtypeStruct((PIECE, stepped, BW), BF16)]
        + [jax.ShapeDtypeStruct((EARLY * N_Y * Q, stepped, BW), BF16)] * N_CORE,
        in_specs=[SMEM, SMEM, SMEM, SMEM, ANY, ANY],
        out_specs=[ANY] * (2 + N_CORE),
        scratch_shapes=[
            pltpu.VMEM((PB, R, BW), BF16),
            pltpu.VMEM((2, PB, BW, BW), BF16),
            pltpu.VMEM((PB, R, BW), BF16),
            pltpu.SemaphoreType.DMA((3, PB // STEP)),
            pltpu.VMEM((PB, straight, BW), BF16),
            pltpu.VMEM((PIECE, stepped, BW), BF16),
            pltpu.VMEM((EARLY * N_Y * Q, stepped, BW), BF16),
            pltpu.VMEM((EARLY * N_Y * Q, stepped, BW), BF16),
            pltpu.SemaphoreType.DMA((2 + EARLY * (1 + N_CORE),)),
        ],
        cost_estimate=pl.CostEstimate(
            flops=4 * PB * R * BW * BW, bytes_accessed=8 * 2**20, transcendentals=0
        ),
        name="col_levels",
    )(row, me, order, ranks, right_sides, factors)


def regroup_kernel(moves, n_in, *refs):
    for source, start, target, place in moves:
        refs[n_in + target][place : place + Q] = refs[source][start : start + Q]


def regroup(rows, moves, n_out, size, pieces, hint=0):
    return pl.pallas_call(
        functools.partial(regroup_kernel, moves, len(pieces)),
        out_shape=[jax.ShapeDtypeStruct((size, rows, BW), BF16)] * n_out,
        in_specs=[VMEM] * len(pieces),
        out_specs=[VMEM] * n_out,
        compiler_params=SMALL,
        cost_estimate=pl.CostEstimate(
            flops=hint, bytes_accessed=4 * n_out * size * rows * BW, transcendentals=0
        ),
        name="regroup",
    )(*pieces)


def held(k, m, e):
    if e == 1:
        return 2, (k * N_Y + m) * Q
    if k == EARLY:
        return 1, m * N_CORE * Q
    return 0, (k * N_Y + m) * Q


def for_core():
    moves = []
    for k in range(N_PLANE):
        for m in range(N_Y):
            place = (k * N_Y + m) * Q
            if k == EARLY:
                moves.append((1, (m * N_CORE + 1) * Q, 0, place))
            else:
                moves.append((0, place, 0, place))
    return moves


def for_y():
    moves = []
    for m in range(1, N_Y):
        for e in range(N_CORE):
            for k in range(N_PLANE):
                moves.append((*held(k, m, e), m - 1, (e * N_PLANE + k) * Q))
    return moves


def for_planes():
    moves = []
    for k in range(N_PLANE):
        for m in range(N_Y):
            for e in range(N_CORE):
                place = (m * N_CORE + e) * Q
                if m == 0:
                    moves.append((*held(k, m, e), k, place))
                else:
                    moves.append((2 + m, (e * N_PLANE + k) * Q, k, place))
    return moves


def mid_kernel(offsets, me_ref, rank_ref, z_ref, w_ref, after_ref, *out_refs):
    for d, out_ref in zip(offsets, out_refs):
        for h in range(N_Z):
            base = (h * N_X + lax.rem(me_ref[0] + d, N_X)) * STEP
            for j in range(STEP):
                inner = masked_dot(z_ref[base + j], w_ref[base + j], rank_ref[base + j])
                out_ref[h * STEP + j] = inner.astype(BF16)


def mid_level(rows, offsets, me, ranks, blocks, factors, after):
    n = len(offsets)
    count = n * N_Z * STEP
    return pl.pallas_call(
        functools.partial(mid_kernel, offsets),
        out_shape=[jax.ShapeDtypeStruct((N_Z * STEP, rows, BW), BF16)] * n,
        in_specs=[SMEM, SMEM, VMEM, VMEM, ANY],
        out_specs=[VMEM] * n,
        compiler_params=SMALL,
        cost_estimate=pl.CostEstimate(
            flops=2 * count * rows * BW * BW + HINT_MID,
            bytes_accessed=count * (4 * rows + 2 * BW) * BW,
            transcendentals=0,
        ),
        name="mid_level",
    )(me, ranks, blocks, factors, after)


def stepped_kernel(row_ref, me_ref, rank_ref, w_ref, *refs):
    pieces, out_refs, inner_buf = refs[:N_PLANE], refs[N_PLANE:-1], refs[-1]
    for k in range(N_PLANE):
        for m in range(N_Y):
            for e in range(N_CORE):
                for i in range(Q):
                    b = (row_ref[0] ^ flip(k, m, e)) * Q + i
                    block = pieces[k][(m * N_CORE + e) * Q + i]
                    inner_buf[b] = masked_dot(block, w_ref[b], rank_ref[b]).astype(BF16)
    for d, out_ref in enumerate(out_refs):
        for h in range(N_Z):
            base = (h * N_X + lax.rem(me_ref[0] + d, N_X)) * STEP
            out_ref[h * STEP : (h + 1) * STEP] = inner_buf[pl.ds(base, STEP)]


def mid_stepped(rows, row, me, ranks, factors, pieces):
    return pl.pallas_call(
        stepped_kernel,
        out_shape=[jax.ShapeDtypeStruct((N_Z * STEP, rows, BW), BF16)] * N_X,
        in_specs=[SMEM, SMEM, SMEM, VMEM] + [VMEM] * N_PLANE,
        out_specs=[VMEM] * N_X,
        scratch_shapes=[pltpu.VMEM((PB, rows, BW), BF16)],
        compiler_params=SMALL,
        cost_estimate=pl.CostEstimate(
            flops=2 * PB * rows * BW * BW + HINT_STEPPED,
            bytes_accessed=PB * (4 * rows + 2 * BW) * BW,
            transcendentals=0,
        ),
        name="mid_stepped",
    )(row, me, ranks, factors, *pieces)


def total_of(refs, half):
    total = refs[0][half].astype(jnp.float32)
    for ref in refs[1:]:
        total = total + ref[half].astype(jnp.float32)
    return total


def sum_kernel(me_ref, *refs):
    half = pl.ds((1 - lax.div(me_ref[0], N_X)) * STEP, STEP)
    refs[N_X][...] = total_of(refs[:N_X], half).astype(BF16)


def sum_other(rows, me, parts):
    return pl.pallas_call(
        sum_kernel,
        out_shape=jax.ShapeDtypeStruct((STEP, rows, BW), BF16),
        in_specs=[SMEM] + [VMEM] * N_X,
        out_specs=VMEM,
        compiler_params=SMALL,
        cost_estimate=pl.CostEstimate(
            flops=4 * STEP * rows * BW, bytes_accessed=10 * STEP * rows * BW, transcendentals=0
        ),
        name="sum_other",
    )(me, *parts)


def row_kernel(me_ref, rank_ref, w_ref, *refs):
    out_ref = refs[-1]
    base = me_ref[0] * OWN
    half = pl.ds(lax.div(me_ref[0], N_X) * STEP, STEP)
    start = 0
    for n, rows in enumerate(CHUNKS):
        near = refs[n * (N_X + 1) : n * (N_X + 1) + N_X]
        far = refs[n * (N_X + 1) + N_X]
        total = total_of(near, half) + far[...].astype(jnp.float32)
        for j in range(0, OWN, 2):
            for i, block in enumerate(pair(total[j], total[j + 1])):
                product = masked_dot(block, w_ref[base + j + i], rank_ref[base + j + i])
                out_ref[j + i, start : start + rows] = product.astype(BF16)
        start += rows


def row_level(me, ranks, factors, parts):
    return pl.pallas_call(
        row_kernel,
        out_shape=jax.ShapeDtypeStruct((OWN, R, BW), BF16),
        in_specs=[SMEM, SMEM, VMEM] + [VMEM] * len(parts),
        out_specs=VMEM,
        compiler_params=SMALL,
        cost_estimate=pl.CostEstimate(
            flops=2 * OWN * R * BW * BW, bytes_accessed=2**20, transcendentals=0
        ),
        name="row_level",
    )(me, ranks, factors, *parts)


def around_x(value, d):
    pairs = [(z * N_X + x, z * N_X + (x + d) % N_X) for z in range(N_Z) for x in range(N_X)]
    return lax.ppermute(value, "col", pairs)


def across_z(value):
    half = N_X * N_Z // 2
    return lax.ppermute(value, "col", [(i, (i + half) % (2 * half)) for i in range(2 * half)])


def across_row(value, k, m, e):
    return lax.ppermute(
        value, "row", [(r, r ^ flip(k, m, e)) for r in range(N_PLANE * N_Y * N_CORE)]
    )


def shards(
    right_sides, col_factors, col_ranks, block_order, mid_factors, mid_ranks, row_factors, row_ranks
):
    me = lax.axis_index("col").astype(jnp.int32).reshape(1)
    row = lax.axis_index("row").astype(jnp.int32).reshape(1)
    ranks, factors = mid_ranks[0], mid_factors[0]
    straight_rows, stepped_rows = CHUNKS
    middle, early, same, other = col_levels(
        row, me, block_order[0], col_ranks, right_sides, col_factors
    )

    early = across_row(early, EARLY, 0, 0)
    regrouped = lax.all_to_all(middle, "row", split_axis=0, concat_axis=0, tiled=True)

    (other,) = regroup(
        stepped_rows, for_core(), 1, PB // N_CORE, [other, early], HINT_CORE
    )
    pieces = [same, early, across_row(other, 0, 0, 1)]
    lines = regroup(stepped_rows, for_y(), N_Y - 1, PIECE, pieces, HINT_Y)
    pieces += [across_row(line, 0, m + 1, 0) for m, line in enumerate(lines)]
    planes = list(regroup(stepped_rows, for_planes(), N_PLANE, PIECE, pieces, HINT_PLANES))
    for k in range(1, EARLY):
        planes[k] = across_row(planes[k], k, 0, 0)

    inner = mid_level(straight_rows, (0, 1, 2, 3), me, ranks, regrouped, factors, planes[0])
    near = [inner[0]] + [around_x(inner[d], d) for d in (2, 1, 3)]
    parts = near + [across_z(sum_other(straight_rows, me, near))]

    inner = mid_stepped(stepped_rows, row, me, ranks, factors, planes)
    near = [inner[0]] + [around_x(inner[d], d) for d in (2, 1, 3)]
    parts += near + [across_z(sum_other(stepped_rows, me, near))]
    return row_level(me, row_ranks, row_factors, parts)


def solution(mesh):
    in_specs = (
        P(("col", "row"), None, None),
        P(None, ("col", "row"), None, None),
        P(None, ("col", "row")),
        P(("col", "row"), None),
        P("col", "row", None, None),
        P("col", "row"),
        P("row", None, None),
        P("row"),
    )
    out_specs = P(("row", "col"), None, None)
    return jax.shard_map(shards, mesh=mesh, in_specs=in_specs, out_specs=out_specs, check_vma=False)
```

```python
import functools

import jax
import jax.numpy as jnp
from jax import lax
from jax.experimental import pallas as pl
from jax.experimental.pallas import tpu as pltpu
from jax.sharding import PartitionSpec as P

BW = 128
HALF = BW // 2
R = 128
PB = 64
STEP = 8
SIDE = STEP // 2
N_X = 4
N_Z = 2
OWN = 8
N_PLANE = 4
N_Y = 4
N_CORE = 2
PLANE = N_Y * N_CORE
Q = 2
PIECE = 16
EARLY = 3
HINT_CORE = 100000000000
HINT_Y = 0
HINT_PLANES = 0
HINT_MID = 100000000000
HINT_JOIN = 0
HINT_STEPPED = 100000000000
CHUNKS = (80, 48)
BF16 = jnp.bfloat16
ANY = pl.BlockSpec(memory_space=pl.ANY)
SMEM = pl.BlockSpec(memory_space=pltpu.SMEM)
VMEM = pl.BlockSpec(memory_space=pltpu.VMEM)
SMALL = pltpu.CompilerParams(vmem_limit_bytes=12 * 2**20)


def masked_dot(blocks, factors, rank):
    product = jnp.dot(blocks, factors, preferred_element_type=jnp.float32)
    lane = lax.broadcasted_iota(jnp.int32, product.shape, 1)
    return jnp.where(lane < rank, product, 0.0)


def pair(even, odd):
    lane = lax.broadcasted_iota(jnp.int32, even.shape, 1)
    front = jnp.where(lane < HALF, even, pltpu.roll(odd, HALF, 1))
    back = jnp.where(lane < HALF, pltpu.roll(even, HALF, 1), odd)
    return front.astype(BF16), back.astype(BF16)


def col_kernel(row_ref, me_ref, order_ref, rank_ref, z_ref, w_ref, *refs):
    out_refs, (z_buf, w_buf, first_buf, sems) = refs[: 2 + N_CORE], refs[2 + N_CORE : 6 + N_CORE]
    straight_buf, early_buf, *bufs = refs[6 + N_CORE : -1]
    out_sems = refs[-1]
    early, late = [], []
    for g in range(PB // STEP):
        part = pl.ds(g * STEP, STEP)
        early.append(pltpu.make_async_copy(z_ref.at[part], z_buf.at[part], sems.at[0, g]))
        early.append(pltpu.make_async_copy(w_ref.at[0, part], w_buf.at[0, part], sems.at[1, g]))
        late.append(pltpu.make_async_copy(w_ref.at[1, part], w_buf.at[1, part], sems.at[2, g]))
    for copy in early + late:
        copy.start()
    for g in range(PB // STEP):
        early[2 * g].wait()
        early[2 * g + 1].wait()
        blocks = range(g * STEP, (g + 1) * STEP)
        first = [masked_dot(z_buf[b], w_buf[0, b], rank_ref[0, b]) for b in blocks]
        for j in range(0, STEP, 2):
            front, back = pair(first[j], first[j + 1])
            first_buf[g * STEP + j] = front
            first_buf[g * STEP + j + 1] = back
    for copy in late:
        copy.wait()
    rows = CHUNKS[0]
    outs = []

    def send(buf, place, out_ref, start, count):
        copy = pltpu.make_async_copy(
            buf.at[pl.ds(place, count)], out_ref.at[pl.ds(start, count)], out_sems.at[len(outs)]
        )
        copy.start()
        outs.append(copy)

    for k in reversed(range(N_PLANE)):
        for m in range(N_Y):
            for e in range(N_CORE):
                for i in range(Q):
                    n = (m * N_CORE + e) * Q + i
                    place = (row_ref[0] ^ flip(k, m, e)) * Q + i
                    b = order_ref[place]
                    middle = masked_dot(first_buf[b], w_buf[1, b], rank_ref[1, b]).astype(BF16)
                    straight_buf[k * PIECE + near_place(row_ref, m, e) + i] = middle[:rows]
                    if k == EARLY:
                        early_buf[n] = middle[rows:]
                    else:
                        bufs[e][(k * N_Y + m) * Q + i] = middle[rows:]
        start = ((row_ref[0] // PLANE) ^ k) * PIECE
        send(straight_buf, k * PIECE, out_refs[0], start, PIECE)
        if k == EARLY:
            send(early_buf, 0, out_refs[1], 0, PIECE)
        else:
            for e in range(N_CORE):
                send(bufs[e], k * N_Y * Q, out_refs[2 + e], k * N_Y * Q, N_Y * Q)
    for copy in outs:
        copy.wait()


def near_place(row_ref, m, e):
    return ((row_ref[0] % PLANE) ^ (m * N_CORE + e)) * Q


def flip(k, m, e):
    return (k * N_Y + m) * N_CORE + e


def col_levels(row, me, order, ranks, right_sides, factors):
    straight, stepped = CHUNKS
    return pl.pallas_call(
        col_kernel,
        out_shape=[jax.ShapeDtypeStruct((PB, straight, BW), BF16)]
        + [jax.ShapeDtypeStruct((PIECE, stepped, BW), BF16)]
        + [jax.ShapeDtypeStruct((EARLY * N_Y * Q, stepped, BW), BF16)] * N_CORE,
        in_specs=[SMEM, SMEM, SMEM, SMEM, ANY, ANY],
        out_specs=[ANY] * (2 + N_CORE),
        scratch_shapes=[
            pltpu.VMEM((PB, R, BW), BF16),
            pltpu.VMEM((2, PB, BW, BW), BF16),
            pltpu.VMEM((PB, R, BW), BF16),
            pltpu.SemaphoreType.DMA((3, PB // STEP)),
            pltpu.VMEM((PB, straight, BW), BF16),
            pltpu.VMEM((PIECE, stepped, BW), BF16),
            pltpu.VMEM((EARLY * N_Y * Q, stepped, BW), BF16),
            pltpu.VMEM((EARLY * N_Y * Q, stepped, BW), BF16),
            pltpu.SemaphoreType.DMA((2 + EARLY * (1 + N_CORE),)),
        ],
        cost_estimate=pl.CostEstimate(
            flops=4 * PB * R * BW * BW, bytes_accessed=8 * 2**20, transcendentals=0
        ),
        name="col_levels",
    )(row, me, order, ranks, right_sides, factors)


def regroup_kernel(moves, n_in, *refs):
    for source, start, target, place in moves:
        refs[n_in + target][place : place + Q] = refs[source][start : start + Q]


def regroup(rows, moves, n_out, size, pieces, hint=0):
    return pl.pallas_call(
        functools.partial(regroup_kernel, moves, len(pieces)),
        out_shape=[jax.ShapeDtypeStruct((size, rows, BW), BF16)] * n_out,
        in_specs=[VMEM] * len(pieces),
        out_specs=[VMEM] * n_out,
        compiler_params=SMALL,
        cost_estimate=pl.CostEstimate(
            flops=hint, bytes_accessed=4 * n_out * size * rows * BW, transcendentals=0
        ),
        name="regroup",
    )(*pieces)


def held(k, m, e):
    if e == 1:
        return 2, (k * N_Y + m) * Q
    if k == EARLY:
        return 1, m * N_CORE * Q
    return 0, (k * N_Y + m) * Q


def for_core():
    moves = []
    for k in range(N_PLANE):
        for m in range(N_Y):
            place = (k * N_Y + m) * Q
            if k == EARLY:
                moves.append((1, (m * N_CORE + 1) * Q, 0, place))
            else:
                moves.append((0, place, 0, place))
    return moves


def for_y():
    moves = []
    for m in range(1, N_Y):
        for e in range(N_CORE):
            for k in range(N_PLANE):
                moves.append((*held(k, m, e), m - 1, (e * N_PLANE + k) * Q))
    return moves


def for_planes():
    moves = []
    for k in range(N_PLANE):
        for m in range(N_Y):
            for e in range(N_CORE):
                place = (m * N_CORE + e) * Q
                if m == 0:
                    moves.append((*held(k, m, e), k, place))
                else:
                    moves.append((2 + m, (e * N_PLANE + k) * Q, k, place))
    return moves


def mid_kernel(me_ref, rank_ref, z_ref, w_ref, after_ref, *out_refs):
    for d in (2, 1, 3, 0):
        for h in range(N_Z):
            base = (h * N_X + lax.rem(me_ref[0] + d, N_X)) * STEP
            for j in range(STEP):
                inner = masked_dot(z_ref[base + j], w_ref[base + j], rank_ref[base + j])
                if d == 2:
                    out_refs[2 + j // SIDE][h * SIDE + j % SIDE] = inner.astype(BF16)
                else:
                    out_refs[d if d < 2 else 4][h * STEP + j] = inner.astype(BF16)


def mid_level(rows, me, ranks, blocks, factors, after):
    whole = jax.ShapeDtypeStruct((N_Z * STEP, rows, BW), BF16)
    side = jax.ShapeDtypeStruct((N_Z * SIDE, rows, BW), BF16)
    return pl.pallas_call(
        mid_kernel,
        out_shape=[whole, whole, side, side, whole],
        in_specs=[SMEM, SMEM, VMEM, VMEM, ANY],
        out_specs=[VMEM] * 5,
        compiler_params=SMALL,
        cost_estimate=pl.CostEstimate(
            flops=2 * PB * rows * BW * BW + HINT_MID,
            bytes_accessed=PB * (4 * rows + 2 * BW) * BW,
            transcendentals=0,
        ),
        name="mid_level",
    )(me, ranks, blocks, factors, after)


def join_kernel(right_ref, left_ref, from_left_ref, from_right_ref, right_out, left_out):
    for h in range(N_Z):
        a, b = h * STEP, h * STEP + SIDE
        sides = slice(h * SIDE, (h + 1) * SIDE)
        first, second = slice(a, a + SIDE), slice(b, b + SIDE)
        right_out[first] = added(right_ref[first], from_left_ref[sides])
        right_out[second] = right_ref[second]
        left_out[first] = left_ref[first]
        left_out[second] = added(left_ref[second], from_right_ref[sides])


def added(a, b):
    return (a.astype(jnp.float32) + b.astype(jnp.float32)).astype(BF16)


def join_sides(rows, right, left, from_left, from_right):
    return pl.pallas_call(
        join_kernel,
        out_shape=[jax.ShapeDtypeStruct((N_Z * STEP, rows, BW), BF16)] * 2,
        in_specs=[VMEM] * 4,
        out_specs=[VMEM] * 2,
        compiler_params=SMALL,
        cost_estimate=pl.CostEstimate(
            flops=STEP * rows * BW + HINT_JOIN,
            bytes_accessed=12 * N_Z * STEP * rows * BW,
            transcendentals=0,
        ),
        name="join_sides",
    )(right, left, from_left, from_right)


def stepped_kernel(row_ref, me_ref, rank_ref, w_ref, *refs):
    pieces, out_refs, inner_buf = refs[:N_PLANE], refs[N_PLANE:-1], refs[-1]
    for k in range(N_PLANE):
        for m in range(N_Y):
            for e in range(N_CORE):
                for i in range(Q):
                    b = (row_ref[0] ^ flip(k, m, e)) * Q + i
                    block = pieces[k][(m * N_CORE + e) * Q + i]
                    inner_buf[b] = masked_dot(block, w_ref[b], rank_ref[b]).astype(BF16)
    for d, out_ref in enumerate(out_refs):
        for h in range(N_Z):
            base = (h * N_X + lax.rem(me_ref[0] + d, N_X)) * STEP
            out_ref[h * STEP : (h + 1) * STEP] = inner_buf[pl.ds(base, STEP)]


def mid_stepped(rows, row, me, ranks, factors, pieces):
    return pl.pallas_call(
        stepped_kernel,
        out_shape=[jax.ShapeDtypeStruct((N_Z * STEP, rows, BW), BF16)] * N_X,
        in_specs=[SMEM, SMEM, SMEM, VMEM] + [VMEM] * N_PLANE,
        out_specs=[VMEM] * N_X,
        scratch_shapes=[pltpu.VMEM((PB, rows, BW), BF16)],
        compiler_params=SMALL,
        cost_estimate=pl.CostEstimate(
            flops=2 * PB * rows * BW * BW + HINT_STEPPED,
            bytes_accessed=PB * (4 * rows + 2 * BW) * BW,
            transcendentals=0,
        ),
        name="mid_stepped",
    )(row, me, ranks, factors, *pieces)


def total_of(refs, half):
    total = refs[0][half].astype(jnp.float32)
    for ref in refs[1:]:
        total = total + ref[half].astype(jnp.float32)
    return total


def sum_kernel(me_ref, *refs):
    half = pl.ds((1 - lax.div(me_ref[0], N_X)) * STEP, STEP)
    refs[-1][...] = total_of(refs[:-1], half).astype(BF16)


def sum_other(rows, me, parts):
    return pl.pallas_call(
        sum_kernel,
        out_shape=jax.ShapeDtypeStruct((STEP, rows, BW), BF16),
        in_specs=[SMEM] + [VMEM] * len(parts),
        out_specs=VMEM,
        compiler_params=SMALL,
        cost_estimate=pl.CostEstimate(
            flops=4 * STEP * rows * BW, bytes_accessed=10 * STEP * rows * BW, transcendentals=0
        ),
        name="sum_other",
    )(me, *parts)


def row_kernel(me_ref, rank_ref, w_ref, *refs):
    out_ref = refs[-1]
    base = me_ref[0] * OWN
    half = pl.ds(lax.div(me_ref[0], N_X) * STEP, STEP)
    start = 0
    for rows, near, far in (
        (CHUNKS[0], refs[:3], refs[3]),
        (CHUNKS[1], refs[4 : 4 + N_X], refs[4 + N_X]),
    ):
        total = total_of(near, half) + far[...].astype(jnp.float32)
        for j in range(0, OWN, 2):
            for i, block in enumerate(pair(total[j], total[j + 1])):
                product = masked_dot(block, w_ref[base + j + i], rank_ref[base + j + i])
                out_ref[j + i, start : start + rows] = product.astype(BF16)
        start += rows


def row_level(me, ranks, factors, parts):
    return pl.pallas_call(
        row_kernel,
        out_shape=jax.ShapeDtypeStruct((OWN, R, BW), BF16),
        in_specs=[SMEM, SMEM, VMEM] + [VMEM] * len(parts),
        out_specs=VMEM,
        compiler_params=SMALL,
        cost_estimate=pl.CostEstimate(
            flops=2 * OWN * R * BW * BW, bytes_accessed=2**20, transcendentals=0
        ),
        name="row_level",
    )(me, ranks, factors, *parts)


def around_x(value, d):
    pairs = [(z * N_X + x, z * N_X + (x + d) % N_X) for z in range(N_Z) for x in range(N_X)]
    return lax.ppermute(value, "col", pairs)


def across_z(value):
    half = N_X * N_Z // 2
    return lax.ppermute(value, "col", [(i, (i + half) % (2 * half)) for i in range(2 * half)])


def across_row(value, k, m, e):
    return lax.ppermute(
        value, "row", [(r, r ^ flip(k, m, e)) for r in range(N_PLANE * N_Y * N_CORE)]
    )


def shards(
    right_sides, col_factors, col_ranks, block_order, mid_factors, mid_ranks, row_factors, row_ranks
):
    me = lax.axis_index("col").astype(jnp.int32).reshape(1)
    row = lax.axis_index("row").astype(jnp.int32).reshape(1)
    ranks, factors = mid_ranks[0], mid_factors[0]
    straight_rows, stepped_rows = CHUNKS
    middle, early, same, other = col_levels(
        row, me, block_order[0], col_ranks, right_sides, col_factors
    )

    early = across_row(early, EARLY, 0, 0)
    regrouped = lax.all_to_all(middle, "row", split_axis=0, concat_axis=0, tiled=True)

    (other,) = regroup(
        stepped_rows, for_core(), 1, PB // N_CORE, [other, early], HINT_CORE
    )
    pieces = [same, early, across_row(other, 0, 0, 1)]
    lines = regroup(stepped_rows, for_y(), N_Y - 1, PIECE, pieces, HINT_Y)
    pieces += [across_row(line, 0, m + 1, 0) for m, line in enumerate(lines)]
    planes = list(regroup(stepped_rows, for_planes(), N_PLANE, PIECE, pieces, HINT_PLANES))
    for k in range(1, EARLY):
        planes[k] = across_row(planes[k], k, 0, 0)

    own, right, first, second, left = mid_level(
        straight_rows, me, ranks, regrouped, factors, planes[0]
    )
    from_left, from_right = around_x(first, 1), around_x(second, 3)
    right, left = join_sides(straight_rows, right, left, from_left, from_right)
    near = [own, around_x(right, 1), around_x(left, 3)]
    parts = near + [across_z(sum_other(straight_rows, me, near))]

    inner = mid_stepped(stepped_rows, row, me, ranks, factors, planes)
    near = [inner[0]] + [around_x(inner[d], d) for d in (2, 1, 3)]
    parts += near + [across_z(sum_other(stepped_rows, me, near))]
    return row_level(me, row_ranks, row_factors, parts)


def solution(mesh):
    in_specs = (
        P(("col", "row"), None, None),
        P(None, ("col", "row"), None, None),
        P(None, ("col", "row")),
        P(("col", "row"), None),
        P("col", "row", None, None),
        P("col", "row"),
        P("row", None, None),
        P("row"),
    )
    out_specs = P(("row", "col"), None, None)
    return jax.shard_map(shards, mesh=mesh, in_specs=in_specs, out_specs=out_specs, check_vma=False)
```

```python
import functools

import jax
import jax.numpy as jnp
from jax import lax
from jax.experimental import pallas as pl
from jax.experimental.pallas import tpu as pltpu
from jax.sharding import PartitionSpec as P

BW = 128
HALF = BW // 2
R = 128
PB = 64
STEP = 8
SIDE = STEP // 2
N_X = 4
N_Z = 2
OWN = 8
N_PLANE = 4
N_Y = 4
N_CORE = 2
PLANE = N_Y * N_CORE
Q = 2
PIECE = 16
EARLY = 3
HINT_CORE = 100000000000
HINT_Y = 0
HINT_PLANES = 0
HINT_MID = 100000000000
HINT_JOIN = 0
HINT_STEPPED = 100000000000
CHUNKS = (80, 48)
BF16 = jnp.bfloat16
ANY = pl.BlockSpec(memory_space=pl.ANY)
SMEM = pl.BlockSpec(memory_space=pltpu.SMEM)
VMEM = pl.BlockSpec(memory_space=pltpu.VMEM)
SMALL = pltpu.CompilerParams(vmem_limit_bytes=12 * 2**20)


def masked_dot(blocks, factors, rank):
    product = jnp.dot(blocks, factors, preferred_element_type=jnp.float32)
    lane = lax.broadcasted_iota(jnp.int32, product.shape, 1)
    return jnp.where(lane < rank, product, 0.0)


def pair(even, odd):
    lane = lax.broadcasted_iota(jnp.int32, even.shape, 1)
    front = jnp.where(lane < HALF, even, pltpu.roll(odd, HALF, 1))
    back = jnp.where(lane < HALF, pltpu.roll(even, HALF, 1), odd)
    return front.astype(BF16), back.astype(BF16)


def col_kernel(row_ref, me_ref, order_ref, rank_ref, z_ref, w_ref, *refs):
    out_refs, (z_buf, w_buf, first_buf, sems) = refs[: 2 + N_CORE], refs[2 + N_CORE : 6 + N_CORE]
    straight_buf, early_buf, *bufs = refs[6 + N_CORE : -1]
    out_sems = refs[-1]
    early, late = [], []
    for g in range(PB // STEP):
        part = pl.ds(g * STEP, STEP)
        early.append(pltpu.make_async_copy(z_ref.at[part], z_buf.at[part], sems.at[0, g]))
        early.append(pltpu.make_async_copy(w_ref.at[0, part], w_buf.at[0, part], sems.at[1, g]))
        late.append(pltpu.make_async_copy(w_ref.at[1, part], w_buf.at[1, part], sems.at[2, g]))
    for copy in early + late:
        copy.start()
    for g in range(PB // STEP):
        early[2 * g].wait()
        early[2 * g + 1].wait()
        blocks = range(g * STEP, (g + 1) * STEP)
        first = [masked_dot(z_buf[b], w_buf[0, b], rank_ref[0, b]) for b in blocks]
        for j in range(0, STEP, 2):
            front, back = pair(first[j], first[j + 1])
            first_buf[g * STEP + j] = front
            first_buf[g * STEP + j + 1] = back
    for copy in late:
        copy.wait()
    rows = CHUNKS[0]
    outs = []

    def send(buf, place, out_ref, start, count):
        copy = pltpu.make_async_copy(
            buf.at[pl.ds(place, count)], out_ref.at[pl.ds(start, count)], out_sems.at[len(outs)]
        )
        copy.start()
        outs.append(copy)

    for k in reversed(range(N_PLANE)):
        for m in range(N_Y):
            for e in range(N_CORE):
                for i in range(Q):
                    n = (m * N_CORE + e) * Q + i
                    place = (row_ref[0] ^ flip(k, m, e)) * Q + i
                    b = order_ref[place]
                    middle = masked_dot(first_buf[b], w_buf[1, b], rank_ref[1, b]).astype(BF16)
                    straight_buf[k * PIECE + near_place(row_ref, m, e) + i] = middle[:rows]
                    if k == EARLY:
                        early_buf[n] = middle[rows:]
                    else:
                        bufs[e][(k * N_Y + m) * Q + i] = middle[rows:]
        start = ((row_ref[0] // PLANE) ^ k) * PIECE
        send(straight_buf, k * PIECE, out_refs[0], start, PIECE)
        if k == EARLY:
            send(early_buf, 0, out_refs[1], 0, PIECE)
        else:
            for e in range(N_CORE):
                send(bufs[e], k * N_Y * Q, out_refs[2 + e], k * N_Y * Q, N_Y * Q)
    for copy in outs:
        copy.wait()


def near_place(row_ref, m, e):
    return ((row_ref[0] % PLANE) ^ (m * N_CORE + e)) * Q


def flip(k, m, e):
    return (k * N_Y + m) * N_CORE + e


def col_levels(row, me, order, ranks, right_sides, factors):
    straight, stepped = CHUNKS
    return pl.pallas_call(
        col_kernel,
        out_shape=[jax.ShapeDtypeStruct((PB, straight, BW), BF16)]
        + [jax.ShapeDtypeStruct((PIECE, stepped, BW), BF16)]
        + [jax.ShapeDtypeStruct((EARLY * N_Y * Q, stepped, BW), BF16)] * N_CORE,
        in_specs=[SMEM, SMEM, SMEM, SMEM, ANY, ANY],
        out_specs=[ANY] * (2 + N_CORE),
        scratch_shapes=[
            pltpu.VMEM((PB, R, BW), BF16),
            pltpu.VMEM((2, PB, BW, BW), BF16),
            pltpu.VMEM((PB, R, BW), BF16),
            pltpu.SemaphoreType.DMA((3, PB // STEP)),
            pltpu.VMEM((PB, straight, BW), BF16),
            pltpu.VMEM((PIECE, stepped, BW), BF16),
            pltpu.VMEM((EARLY * N_Y * Q, stepped, BW), BF16),
            pltpu.VMEM((EARLY * N_Y * Q, stepped, BW), BF16),
            pltpu.SemaphoreType.DMA((2 + EARLY * (1 + N_CORE),)),
        ],
        cost_estimate=pl.CostEstimate(
            flops=4 * PB * R * BW * BW, bytes_accessed=8 * 2**20, transcendentals=0
        ),
        name="col_levels",
    )(row, me, order, ranks, right_sides, factors)


def regroup_kernel(moves, n_in, *refs):
    for source, start, target, place in moves:
        refs[n_in + target][place : place + Q] = refs[source][start : start + Q]


def regroup(rows, moves, n_out, size, pieces, hint=0, after=()):
    return pl.pallas_call(
        functools.partial(regroup_kernel, moves, len(pieces) + len(after)),
        out_shape=[jax.ShapeDtypeStruct((size, rows, BW), BF16)] * n_out,
        in_specs=[VMEM] * len(pieces) + [ANY] * len(after),
        out_specs=[VMEM] * n_out,
        compiler_params=SMALL,
        cost_estimate=pl.CostEstimate(
            flops=hint, bytes_accessed=4 * n_out * size * rows * BW, transcendentals=0
        ),
        name="regroup",
    )(*pieces, *after)


def held(k, m, e):
    if e == 1:
        return 2, (k * N_Y + m) * Q
    if k == EARLY:
        return 1, m * N_CORE * Q
    return 0, (k * N_Y + m) * Q


def for_core():
    moves = []
    for k in range(N_PLANE):
        for m in range(N_Y):
            place = (k * N_Y + m) * Q
            if k == EARLY:
                moves.append((1, (m * N_CORE + 1) * Q, 0, place))
            else:
                moves.append((0, place, 0, place))
    return moves


def for_y():
    moves = []
    for m in range(1, N_Y):
        for e in range(N_CORE):
            for k in range(N_PLANE):
                moves.append((*held(k, m, e), m - 1, (e * N_PLANE + k) * Q))
    return moves


def for_planes():
    moves = []
    for k in range(N_PLANE):
        for m in range(N_Y):
            for e in range(N_CORE):
                place = (m * N_CORE + e) * Q
                if m == 0:
                    moves.append((*held(k, m, e), k, place))
                else:
                    moves.append((2 + m, (e * N_PLANE + k) * Q, k, place))
    return moves


def pick_kernel(me_ref, w_ref, far_ref, near_ref):
    for n, d in enumerate((2, 1, 3, 0)):
        for h in range(N_Z):
            base = (h * N_X + lax.rem(me_ref[0] + d, N_X)) * STEP
            out_ref, slot = (far_ref, h) if n == 0 else (near_ref, (n - 1) * N_Z + h)
            out_ref[slot * STEP : (slot + 1) * STEP] = w_ref[pl.ds(base, STEP)]


def pick_factors(me, factors):
    count = N_Z * STEP
    return pl.pallas_call(
        pick_kernel,
        out_shape=[
            jax.ShapeDtypeStruct((count, BW, BW), BF16),
            jax.ShapeDtypeStruct((PB - count, BW, BW), BF16),
        ],
        in_specs=[SMEM, VMEM],
        out_specs=[VMEM] * 2,
        compiler_params=SMALL,
        cost_estimate=pl.CostEstimate(
            flops=0, bytes_accessed=4 * PB * BW * BW, transcendentals=0
        ),
        name="pick_factors",
    )(me, factors)


def far_kernel(me_ref, rank_ref, z_ref, w_ref, after_ref, first_ref, second_ref):
    for h in range(N_Z):
        base = (h * N_X + lax.rem(me_ref[0] + 2, N_X)) * STEP
        for j in range(STEP):
            inner = masked_dot(z_ref[base + j], w_ref[h * STEP + j], rank_ref[base + j])
            out_ref = first_ref if j < SIDE else second_ref
            out_ref[h * SIDE + j % SIDE] = inner.astype(BF16)


def near_kernel(me_ref, rank_ref, z_ref, w_ref, after_ref, *out_refs):
    for n, d in enumerate((1, 3, 0)):
        for h in range(N_Z):
            base = (h * N_X + lax.rem(me_ref[0] + d, N_X)) * STEP
            for j in range(STEP):
                factors = w_ref[(n * N_Z + h) * STEP + j]
                inner = masked_dot(z_ref[base + j], factors, rank_ref[base + j])
                out_refs[n][h * STEP + j] = inner.astype(BF16)


def mid_part(kernel, name, rows, sizes, me, ranks, blocks, factors, after):
    count = factors.shape[0]
    return pl.pallas_call(
        kernel,
        out_shape=[jax.ShapeDtypeStruct((size, rows, BW), BF16) for size in sizes],
        in_specs=[SMEM, SMEM, VMEM, VMEM, ANY],
        out_specs=[VMEM] * len(sizes),
        compiler_params=SMALL,
        cost_estimate=pl.CostEstimate(
            flops=2 * count * rows * BW * BW + HINT_MID,
            bytes_accessed=count * (4 * rows + 2 * BW) * BW,
            transcendentals=0,
        ),
        name=name,
    )(me, ranks, blocks, factors, after)


def join_kernel(right_ref, left_ref, from_left_ref, from_right_ref, right_out, left_out):
    for h in range(N_Z):
        a, b = h * STEP, h * STEP + SIDE
        sides = slice(h * SIDE, (h + 1) * SIDE)
        first, second = slice(a, a + SIDE), slice(b, b + SIDE)
        right_out[first] = added(right_ref[first], from_left_ref[sides])
        right_out[second] = right_ref[second]
        left_out[first] = left_ref[first]
        left_out[second] = added(left_ref[second], from_right_ref[sides])


def added(a, b):
    return (a.astype(jnp.float32) + b.astype(jnp.float32)).astype(BF16)


def join_sides(rows, right, left, from_left, from_right):
    return pl.pallas_call(
        join_kernel,
        out_shape=[jax.ShapeDtypeStruct((N_Z * STEP, rows, BW), BF16)] * 2,
        in_specs=[VMEM] * 4,
        out_specs=[VMEM] * 2,
        compiler_params=SMALL,
        cost_estimate=pl.CostEstimate(
            flops=STEP * rows * BW + HINT_JOIN,
            bytes_accessed=12 * N_Z * STEP * rows * BW,
            transcendentals=0,
        ),
        name="join_sides",
    )(right, left, from_left, from_right)


def stepped_kernel(row_ref, me_ref, rank_ref, w_ref, *refs):
    pieces, out_refs, inner_buf = refs[:N_PLANE], refs[N_PLANE:-1], refs[-1]
    for k in range(N_PLANE):
        for m in range(N_Y):
            for e in range(N_CORE):
                for i in range(Q):
                    b = (row_ref[0] ^ flip(k, m, e)) * Q + i
                    block = pieces[k][(m * N_CORE + e) * Q + i]
                    inner_buf[b] = masked_dot(block, w_ref[b], rank_ref[b]).astype(BF16)
    for d, out_ref in enumerate(out_refs):
        for h in range(N_Z):
            base = (h * N_X + lax.rem(me_ref[0] + d, N_X)) * STEP
            out_ref[h * STEP : (h + 1) * STEP] = inner_buf[pl.ds(base, STEP)]


def mid_stepped(rows, row, me, ranks, factors, pieces):
    return pl.pallas_call(
        stepped_kernel,
        out_shape=[jax.ShapeDtypeStruct((N_Z * STEP, rows, BW), BF16)] * N_X,
        in_specs=[SMEM, SMEM, SMEM, VMEM] + [VMEM] * N_PLANE,
        out_specs=[VMEM] * N_X,
        scratch_shapes=[pltpu.VMEM((PB, rows, BW), BF16)],
        compiler_params=SMALL,
        cost_estimate=pl.CostEstimate(
            flops=2 * PB * rows * BW * BW + HINT_STEPPED,
            bytes_accessed=PB * (4 * rows + 2 * BW) * BW,
            transcendentals=0,
        ),
        name="mid_stepped",
    )(row, me, ranks, factors, *pieces)


def total_of(refs, half):
    total = refs[0][half].astype(jnp.float32)
    for ref in refs[1:]:
        total = total + ref[half].astype(jnp.float32)
    return total


def sum_kernel(me_ref, *refs):
    half = pl.ds((1 - lax.div(me_ref[0], N_X)) * STEP, STEP)
    refs[-1][...] = total_of(refs[:-1], half).astype(BF16)


def sum_other(rows, me, parts):
    return pl.pallas_call(
        sum_kernel,
        out_shape=jax.ShapeDtypeStruct((STEP, rows, BW), BF16),
        in_specs=[SMEM] + [VMEM] * len(parts),
        out_specs=VMEM,
        compiler_params=SMALL,
        cost_estimate=pl.CostEstimate(
            flops=4 * STEP * rows * BW, bytes_accessed=10 * STEP * rows * BW, transcendentals=0
        ),
        name="sum_other",
    )(me, *parts)


def row_kernel(me_ref, rank_ref, w_ref, *refs):
    out_ref = refs[-1]
    base = me_ref[0] * OWN
    half = pl.ds(lax.div(me_ref[0], N_X) * STEP, STEP)
    start = 0
    for rows, near, far in (
        (CHUNKS[0], refs[:3], refs[3]),
        (CHUNKS[1], refs[4 : 4 + N_X], refs[4 + N_X]),
    ):
        total = total_of(near, half) + far[...].astype(jnp.float32)
        for j in range(0, OWN, 2):
            for i, block in enumerate(pair(total[j], total[j + 1])):
                product = masked_dot(block, w_ref[base + j + i], rank_ref[base + j + i])
                out_ref[j + i, start : start + rows] = product.astype(BF16)
        start += rows


def row_level(me, ranks, factors, parts):
    return pl.pallas_call(
        row_kernel,
        out_shape=jax.ShapeDtypeStruct((OWN, R, BW), BF16),
        in_specs=[SMEM, SMEM, VMEM] + [VMEM] * len(parts),
        out_specs=VMEM,
        compiler_params=SMALL,
        cost_estimate=pl.CostEstimate(
            flops=2 * OWN * R * BW * BW, bytes_accessed=2**20, transcendentals=0
        ),
        name="row_level",
    )(me, ranks, factors, *parts)


def around_x(value, d):
    pairs = [(z * N_X + x, z * N_X + (x + d) % N_X) for z in range(N_Z) for x in range(N_X)]
    return lax.ppermute(value, "col", pairs)


def across_z(value):
    half = N_X * N_Z // 2
    return lax.ppermute(value, "col", [(i, (i + half) % (2 * half)) for i in range(2 * half)])


def across_row(value, k, m, e):
    return lax.ppermute(
        value, "row", [(r, r ^ flip(k, m, e)) for r in range(N_PLANE * N_Y * N_CORE)]
    )


def shards(
    right_sides, col_factors, col_ranks, block_order, mid_factors, mid_ranks, row_factors, row_ranks
):
    me = lax.axis_index("col").astype(jnp.int32).reshape(1)
    row = lax.axis_index("row").astype(jnp.int32).reshape(1)
    ranks, factors = mid_ranks[0], mid_factors[0]
    straight_rows, stepped_rows = CHUNKS
    middle, early, same, other = col_levels(
        row, me, block_order[0], col_ranks, right_sides, col_factors
    )

    early = across_row(early, EARLY, 0, 0)
    regrouped = lax.all_to_all(middle, "row", split_axis=0, concat_axis=0, tiled=True)

    (other,) = regroup(
        stepped_rows, for_core(), 1, PB // N_CORE, [other, early], HINT_CORE
    )
    pieces = [same, early, across_row(other, 0, 0, 1)]
    lines = regroup(stepped_rows, for_y(), N_Y - 1, PIECE, pieces, HINT_Y)
    pieces += [across_row(line, 0, m + 1, 0) for m, line in enumerate(lines)]
    far_factors, near_factors = pick_factors(me, factors)
    planes = list(
        regroup(
            stepped_rows, for_planes(), N_PLANE, PIECE, pieces, HINT_PLANES, [far_factors]
        )
    )
    for k in range(1, EARLY):
        planes[k] = across_row(planes[k], k, 0, 0)

    first, second = mid_part(
        far_kernel, "mid_far", straight_rows, [STEP, STEP], me, ranks, regrouped, far_factors,
        planes[0],
    )
    right, left, own = mid_part(
        near_kernel, "mid_near", straight_rows, [N_Z * STEP] * 3, me, ranks, regrouped,
        near_factors, first,
    )
    from_left, from_right = around_x(first, 1), around_x(second, 3)
    right, left = join_sides(straight_rows, right, left, from_left, from_right)
    near = [own, around_x(right, 1), around_x(left, 3)]
    parts = near + [across_z(sum_other(straight_rows, me, near))]

    inner = mid_stepped(stepped_rows, row, me, ranks, factors, planes)
    near = [inner[0]] + [around_x(inner[d], d) for d in (2, 1, 3)]
    parts += near + [across_z(sum_other(stepped_rows, me, near))]
    return row_level(me, row_ranks, row_factors, parts)


def solution(mesh):
    in_specs = (
        P(("col", "row"), None, None),
        P(None, ("col", "row"), None, None),
        P(None, ("col", "row")),
        P(("col", "row"), None),
        P("col", "row", None, None),
        P("col", "row"),
        P("row", None, None),
        P("row"),
    )
    out_specs = P(("row", "col"), None, None)
    return jax.shard_map(shards, mesh=mesh, in_specs=in_specs, out_specs=out_specs, check_vma=False)
```

```python
import functools

import jax
import jax.numpy as jnp
from jax import lax
from jax.experimental import pallas as pl
from jax.experimental.pallas import tpu as pltpu
from jax.sharding import PartitionSpec as P

BW = 128
HALF = BW // 2
R = 128
PB = 64
STEP = 8
SIDE = STEP // 2
N_X = 4
N_Z = 2
OWN = 8
N_PLANE = 4
N_Y = 4
N_CORE = 2
PLANE = N_Y * N_CORE
Q = 2
PIECE = 16
EARLY = 3
HINT_CORE = 100000000000
HINT_Y = 0
HINT_PLANES = 0
HINT_MID = 100000000000
HINT_JOIN = 0
HINT_STEPPED = 100000000000
CHUNKS = (80, 48)
BF16 = jnp.bfloat16
ANY = pl.BlockSpec(memory_space=pl.ANY)
SMEM = pl.BlockSpec(memory_space=pltpu.SMEM)
VMEM = pl.BlockSpec(memory_space=pltpu.VMEM)
SMALL = pltpu.CompilerParams(vmem_limit_bytes=12 * 2**20)


def masked_dot(blocks, factors, rank):
    product = jnp.dot(blocks, factors, preferred_element_type=jnp.float32)
    lane = lax.broadcasted_iota(jnp.int32, product.shape, 1)
    return jnp.where(lane < rank, product, 0.0)


def pair(even, odd):
    lane = lax.broadcasted_iota(jnp.int32, even.shape, 1)
    front = jnp.where(lane < HALF, even, pltpu.roll(odd, HALF, 1))
    back = jnp.where(lane < HALF, pltpu.roll(even, HALF, 1), odd)
    return front.astype(BF16), back.astype(BF16)


def col_kernel(row_ref, me_ref, order_ref, rank_ref, z_ref, w_ref, *refs):
    out_refs, (z_buf, w_buf, first_buf, sems) = refs[: 2 + N_CORE], refs[2 + N_CORE : 6 + N_CORE]
    straight_buf, early_buf, *bufs = refs[6 + N_CORE : -1]
    out_sems = refs[-1]
    early, late = [], []
    for g in range(PB // STEP):
        part = pl.ds(g * STEP, STEP)
        early.append(pltpu.make_async_copy(z_ref.at[part], z_buf.at[part], sems.at[0, g]))
        early.append(pltpu.make_async_copy(w_ref.at[0, part], w_buf.at[0, part], sems.at[1, g]))
        late.append(pltpu.make_async_copy(w_ref.at[1, part], w_buf.at[1, part], sems.at[2, g]))
    for copy in early + late:
        copy.start()
    for g in range(PB // STEP):
        early[2 * g].wait()
        early[2 * g + 1].wait()
        blocks = range(g * STEP, (g + 1) * STEP)
        first = [masked_dot(z_buf[b], w_buf[0, b], rank_ref[0, b]) for b in blocks]
        for j in range(0, STEP, 2):
            front, back = pair(first[j], first[j + 1])
            first_buf[g * STEP + j] = front
            first_buf[g * STEP + j + 1] = back
    for copy in late:
        copy.wait()
    rows = CHUNKS[0]
    outs = []

    def send(buf, place, out_ref, start, count):
        copy = pltpu.make_async_copy(
            buf.at[pl.ds(place, count)], out_ref.at[pl.ds(start, count)], out_sems.at[len(outs)]
        )
        copy.start()
        outs.append(copy)

    for k in reversed(range(N_PLANE)):
        for m in range(N_Y):
            for e in range(N_CORE):
                for i in range(Q):
                    n = (m * N_CORE + e) * Q + i
                    place = (row_ref[0] ^ flip(k, m, e)) * Q + i
                    b = order_ref[place]
                    middle = masked_dot(first_buf[b], w_buf[1, b], rank_ref[1, b]).astype(BF16)
                    straight_buf[k * PIECE + near_place(row_ref, m, e) + i] = middle[:rows]
                    if k == EARLY:
                        early_buf[n] = middle[rows:]
                    else:
                        bufs[e][(k * N_Y + m) * Q + i] = middle[rows:]
        start = ((row_ref[0] // PLANE) ^ k) * PIECE
        send(straight_buf, k * PIECE, out_refs[0], start, PIECE)
        if k == EARLY:
            send(early_buf, 0, out_refs[1], 0, PIECE)
        else:
            for e in range(N_CORE):
                send(bufs[e], k * N_Y * Q, out_refs[2 + e], k * N_Y * Q, N_Y * Q)
    for copy in outs:
        copy.wait()


def near_place(row_ref, m, e):
    return ((row_ref[0] % PLANE) ^ (m * N_CORE + e)) * Q


def flip(k, m, e):
    return (k * N_Y + m) * N_CORE + e


def col_levels(row, me, order, ranks, right_sides, factors):
    straight, stepped = CHUNKS
    return pl.pallas_call(
        col_kernel,
        out_shape=[jax.ShapeDtypeStruct((PB, straight, BW), BF16)]
        + [jax.ShapeDtypeStruct((PIECE, stepped, BW), BF16)]
        + [jax.ShapeDtypeStruct((EARLY * N_Y * Q, stepped, BW), BF16)] * N_CORE,
        in_specs=[SMEM, SMEM, SMEM, SMEM, ANY, ANY],
        out_specs=[ANY] * (2 + N_CORE),
        scratch_shapes=[
            pltpu.VMEM((PB, R, BW), BF16),
            pltpu.VMEM((2, PB, BW, BW), BF16),
            pltpu.VMEM((PB, R, BW), BF16),
            pltpu.SemaphoreType.DMA((3, PB // STEP)),
            pltpu.VMEM((PB, straight, BW), BF16),
            pltpu.VMEM((PIECE, stepped, BW), BF16),
            pltpu.VMEM((EARLY * N_Y * Q, stepped, BW), BF16),
            pltpu.VMEM((EARLY * N_Y * Q, stepped, BW), BF16),
            pltpu.SemaphoreType.DMA((2 + EARLY * (1 + N_CORE),)),
        ],
        cost_estimate=pl.CostEstimate(
            flops=4 * PB * R * BW * BW, bytes_accessed=8 * 2**20, transcendentals=0
        ),
        name="col_levels",
    )(row, me, order, ranks, right_sides, factors)


def regroup_kernel(moves, n_in, *refs):
    for source, start, target, place in moves:
        refs[n_in + target][place : place + Q] = refs[source][start : start + Q]


def regroup(rows, moves, n_out, size, pieces, hint=0, after=()):
    return pl.pallas_call(
        functools.partial(regroup_kernel, moves, len(pieces) + len(after)),
        out_shape=[jax.ShapeDtypeStruct((size, rows, BW), BF16)] * n_out,
        in_specs=[VMEM] * len(pieces) + [ANY] * len(after),
        out_specs=[VMEM] * n_out,
        compiler_params=SMALL,
        cost_estimate=pl.CostEstimate(
            flops=hint, bytes_accessed=4 * n_out * size * rows * BW, transcendentals=0
        ),
        name="regroup",
    )(*pieces, *after)


def held(k, m, e):
    if e == 1:
        return 2, (k * N_Y + m) * Q
    if k == EARLY:
        return 1, m * N_CORE * Q
    return 0, (k * N_Y + m) * Q


def for_core():
    moves = []
    for k in range(N_PLANE):
        for m in range(N_Y):
            place = (k * N_Y + m) * Q
            if k == EARLY:
                moves.append((1, (m * N_CORE + 1) * Q, 0, place))
            else:
                moves.append((0, place, 0, place))
    return moves


def for_y():
    moves = []
    for m in range(1, N_Y):
        for e in range(N_CORE):
            for k in range(N_PLANE):
                moves.append((*held(k, m, e), m - 1, (e * N_PLANE + k) * Q))
    return moves


def for_planes():
    moves = []
    for k in range(N_PLANE):
        for m in range(N_Y):
            for e in range(N_CORE):
                place = (m * N_CORE + e) * Q
                if m == 0:
                    moves.append((*held(k, m, e), k, place))
                else:
                    moves.append((2 + m, (e * N_PLANE + k) * Q, k, place))
    return moves


def pick_kernel(me_ref, w_ref, far_ref, near_ref):
    for n, d in enumerate((2, 1, 3, 0)):
        for h in range(N_Z):
            base = (h * N_X + lax.rem(me_ref[0] + d, N_X)) * STEP
            out_ref, slot = (far_ref, h) if n == 0 else (near_ref, (n - 1) * N_Z + h)
            out_ref[slot * STEP : (slot + 1) * STEP] = w_ref[pl.ds(base, STEP)]


def pick_factors(me, factors):
    count = N_Z * STEP
    return pl.pallas_call(
        pick_kernel,
        out_shape=[
            jax.ShapeDtypeStruct((count, BW, BW), BF16),
            jax.ShapeDtypeStruct((PB - count, BW, BW), BF16),
        ],
        in_specs=[SMEM, VMEM],
        out_specs=[VMEM] * 2,
        compiler_params=SMALL,
        cost_estimate=pl.CostEstimate(
            flops=0, bytes_accessed=4 * PB * BW * BW, transcendentals=0
        ),
        name="pick_factors",
    )(me, factors)


def far_kernel(me_ref, rank_ref, z_ref, w_ref, after_ref, first_ref, second_ref):
    for h in range(N_Z):
        base = (h * N_X + lax.rem(me_ref[0] + 2, N_X)) * STEP
        for j in range(STEP):
            inner = masked_dot(z_ref[base + j], w_ref[h * STEP + j], rank_ref[base + j])
            out_ref = first_ref if j < SIDE else second_ref
            out_ref[h * SIDE + j % SIDE] = inner.astype(BF16)


def near_kernel(me_ref, rank_ref, z_ref, w_ref, after_ref, *out_refs):
    for n, d in enumerate((1, 3, 0)):
        for h in range(N_Z):
            base = (h * N_X + lax.rem(me_ref[0] + d, N_X)) * STEP
            for j in range(STEP):
                factors = w_ref[(n * N_Z + h) * STEP + j]
                inner = masked_dot(z_ref[base + j], factors, rank_ref[base + j])
                out_refs[n][h * STEP + j] = inner.astype(BF16)


def mid_part(kernel, name, rows, sizes, me, ranks, blocks, factors, after):
    count = factors.shape[0]
    return pl.pallas_call(
        kernel,
        out_shape=[jax.ShapeDtypeStruct((size, rows, BW), BF16) for size in sizes],
        in_specs=[SMEM, SMEM, VMEM, VMEM, ANY],
        out_specs=[VMEM] * len(sizes),
        compiler_params=SMALL,
        cost_estimate=pl.CostEstimate(
            flops=2 * count * rows * BW * BW + HINT_MID,
            bytes_accessed=count * (4 * rows + 2 * BW) * BW,
            transcendentals=0,
        ),
        name=name,
    )(me, ranks, blocks, factors, after)


def join_kernel(right_ref, left_ref, from_left_ref, from_right_ref, right_out, left_out):
    for h in range(N_Z):
        a, b = h * STEP, h * STEP + SIDE
        sides = slice(h * SIDE, (h + 1) * SIDE)
        first, second = slice(a, a + SIDE), slice(b, b + SIDE)
        right_out[first] = added(right_ref[first], from_left_ref[sides])
        right_out[second] = right_ref[second]
        left_out[first] = left_ref[first]
        left_out[second] = added(left_ref[second], from_right_ref[sides])


def added(a, b):
    return (a.astype(jnp.float32) + b.astype(jnp.float32)).astype(BF16)


def join_sides(rows, right, left, from_left, from_right):
    return pl.pallas_call(
        join_kernel,
        out_shape=[jax.ShapeDtypeStruct((N_Z * STEP, rows, BW), BF16)] * 2,
        in_specs=[VMEM] * 4,
        out_specs=[VMEM] * 2,
        compiler_params=SMALL,
        cost_estimate=pl.CostEstimate(
            flops=STEP * rows * BW + HINT_JOIN,
            bytes_accessed=12 * N_Z * STEP * rows * BW,
            transcendentals=0,
        ),
        name="join_sides",
    )(right, left, from_left, from_right)


def stepped_kernel(row_ref, me_ref, rank_ref, far_ref, near_ref, *refs):
    pieces, out_refs, block_buf = refs[:N_PLANE], refs[N_PLANE:-1], refs[-1]
    for k in range(N_PLANE):
        for m in range(N_Y):
            for e in range(N_CORE):
                b = (row_ref[0] ^ flip(k, m, e)) * Q
                at = (m * N_CORE + e) * Q
                block_buf[pl.ds(b, Q)] = pieces[k][at : at + Q]
    for n, d in enumerate((2, 1, 3, 0)):
        for h in range(N_Z):
            base = (h * N_X + lax.rem(me_ref[0] + d, N_X)) * STEP
            w_ref, slot = (far_ref, h) if n == 0 else (near_ref, (n - 1) * N_Z + h)
            for j in range(STEP):
                factors = w_ref[slot * STEP + j]
                inner = masked_dot(block_buf[base + j], factors, rank_ref[base + j])
                out_refs[d][h * STEP + j] = inner.astype(BF16)


def mid_stepped(rows, row, me, ranks, far_factors, near_factors, pieces):
    return pl.pallas_call(
        stepped_kernel,
        out_shape=[jax.ShapeDtypeStruct((N_Z * STEP, rows, BW), BF16)] * N_X,
        in_specs=[SMEM, SMEM, SMEM, VMEM, VMEM] + [VMEM] * N_PLANE,
        out_specs=[VMEM] * N_X,
        scratch_shapes=[pltpu.VMEM((PB, rows, BW), BF16)],
        compiler_params=SMALL,
        cost_estimate=pl.CostEstimate(
            flops=2 * PB * rows * BW * BW + HINT_STEPPED,
            bytes_accessed=PB * (4 * rows + 2 * BW) * BW,
            transcendentals=0,
        ),
        name="mid_stepped",
    )(row, me, ranks, far_factors, near_factors, *pieces)


def total_of(refs, half):
    total = refs[0][half].astype(jnp.float32)
    for ref in refs[1:]:
        total = total + ref[half].astype(jnp.float32)
    return total


def sum_kernel(me_ref, *refs):
    half = pl.ds((1 - lax.div(me_ref[0], N_X)) * STEP, STEP)
    refs[-1][...] = total_of(refs[:-1], half).astype(BF16)


def sum_other(rows, me, parts):
    return pl.pallas_call(
        sum_kernel,
        out_shape=jax.ShapeDtypeStruct((STEP, rows, BW), BF16),
        in_specs=[SMEM] + [VMEM] * len(parts),
        out_specs=VMEM,
        compiler_params=SMALL,
        cost_estimate=pl.CostEstimate(
            flops=4 * STEP * rows * BW, bytes_accessed=10 * STEP * rows * BW, transcendentals=0
        ),
        name="sum_other",
    )(me, *parts)


def row_kernel(me_ref, rank_ref, w_ref, *refs):
    out_ref, out_buf, sems = refs[-3:]
    base = me_ref[0] * OWN
    half = pl.ds(lax.div(me_ref[0], N_X) * STEP, STEP)
    totals = []
    for near, far in ((refs[:3], refs[3]), (refs[4 : 4 + N_X], refs[4 + N_X])):
        totals.append(total_of(near, half) + far[...].astype(jnp.float32))
    copies = []
    for j in range(0, OWN, 2):
        start = 0
        for total, rows in zip(totals, CHUNKS):
            for i, block in enumerate(pair(total[j], total[j + 1])):
                product = masked_dot(block, w_ref[base + j + i], rank_ref[base + j + i])
                out_buf[j + i, start : start + rows] = product.astype(BF16)
            start += rows
        two = pl.ds(j, 2)
        copies.append(pltpu.make_async_copy(out_buf.at[two], out_ref.at[two], sems.at[j // 2]))
        copies[-1].start()
    for copy in copies:
        copy.wait()


def row_level(me, ranks, factors, parts):
    return pl.pallas_call(
        row_kernel,
        out_shape=jax.ShapeDtypeStruct((OWN, R, BW), BF16),
        in_specs=[SMEM, SMEM, VMEM] + [VMEM] * len(parts),
        out_specs=ANY,
        scratch_shapes=[
            pltpu.VMEM((OWN, R, BW), BF16),
            pltpu.SemaphoreType.DMA((OWN // 2,)),
        ],
        compiler_params=SMALL,
        cost_estimate=pl.CostEstimate(
            flops=2 * OWN * R * BW * BW, bytes_accessed=2**20, transcendentals=0
        ),
        name="row_level",
    )(me, ranks, factors, *parts)


def around_x(value, d):
    pairs = [(z * N_X + x, z * N_X + (x + d) % N_X) for z in range(N_Z) for x in range(N_X)]
    return lax.ppermute(value, "col", pairs)


def across_z(value):
    half = N_X * N_Z // 2
    return lax.ppermute(value, "col", [(i, (i + half) % (2 * half)) for i in range(2 * half)])


def across_row(value, k, m, e):
    return lax.ppermute(
        value, "row", [(r, r ^ flip(k, m, e)) for r in range(N_PLANE * N_Y * N_CORE)]
    )


def shards(
    right_sides, col_factors, col_ranks, block_order, mid_factors, mid_ranks, row_factors, row_ranks
):
    me = lax.axis_index("col").astype(jnp.int32).reshape(1)
    row = lax.axis_index("row").astype(jnp.int32).reshape(1)
    ranks, factors = mid_ranks[0], mid_factors[0]
    straight_rows, stepped_rows = CHUNKS
    middle, early, same, other = col_levels(
        row, me, block_order[0], col_ranks, right_sides, col_factors
    )

    early = across_row(early, EARLY, 0, 0)
    regrouped = lax.all_to_all(middle, "row", split_axis=0, concat_axis=0, tiled=True)

    (other,) = regroup(
        stepped_rows, for_core(), 1, PB // N_CORE, [other, early], HINT_CORE
    )
    pieces = [same, early, across_row(other, 0, 0, 1)]
    lines = regroup(stepped_rows, for_y(), N_Y - 1, PIECE, pieces, HINT_Y)
    pieces += [across_row(line, 0, m + 1, 0) for m, line in enumerate(lines)]
    far_factors, near_factors = pick_factors(me, factors)
    planes = list(
        regroup(
            stepped_rows, for_planes(), N_PLANE, PIECE, pieces, HINT_PLANES, [far_factors]
        )
    )
    for k in range(1, EARLY):
        planes[k] = across_row(planes[k], k, 0, 0)

    first, second = mid_part(
        far_kernel, "mid_far", straight_rows, [STEP, STEP], me, ranks, regrouped, far_factors,
        planes[0],
    )
    right, left, own = mid_part(
        near_kernel, "mid_near", straight_rows, [N_Z * STEP] * 3, me, ranks, regrouped,
        near_factors, first,
    )
    from_left, from_right = around_x(first, 1), around_x(second, 3)
    right, left = join_sides(straight_rows, right, left, from_left, from_right)
    near = [own, around_x(right, 1), around_x(left, 3)]
    parts = near + [across_z(sum_other(straight_rows, me, near))]

    inner = mid_stepped(
        stepped_rows, row, me, ranks, far_factors, near_factors, planes
    )
    near = [inner[0]] + [around_x(inner[d], d) for d in (2, 1, 3)]
    parts += near + [across_z(sum_other(stepped_rows, me, near))]
    return row_level(me, row_ranks, row_factors, parts)


def solution(mesh):
    in_specs = (
        P(("col", "row"), None, None),
        P(None, ("col", "row"), None, None),
        P(None, ("col", "row")),
        P(("col", "row"), None),
        P("col", "row", None, None),
        P("col", "row"),
        P("row", None, None),
        P("row"),
    )
    out_specs = P(("row", "col"), None, None)
    return jax.shard_map(shards, mesh=mesh, in_specs=in_specs, out_specs=out_specs, check_vma=False)
```

```python
import functools

import jax
import jax.numpy as jnp
from jax import lax
from jax.experimental import pallas as pl
from jax.experimental.pallas import tpu as pltpu
from jax.sharding import PartitionSpec as P

BW = 128
HALF = BW // 2
R = 128
PB = 64
STEP = 8
SIDE = STEP // 2
N_X = 4
N_Z = 2
OWN = 8
N_PLANE = 4
N_Y = 4
N_CORE = 2
PLANE = N_Y * N_CORE
Q = 2
PIECE = 16
EARLY = 3
HINT_CORE = 100000000000
HINT_Y = 0
HINT_PLANES = 0
HINT_MID = 100000000000
HINT_JOIN = 0
HINT_STEPPED = 100000000000
CHUNKS = (80, 48)
BF16 = jnp.bfloat16
ANY = pl.BlockSpec(memory_space=pl.ANY)
SMEM = pl.BlockSpec(memory_space=pltpu.SMEM)
VMEM = pl.BlockSpec(memory_space=pltpu.VMEM)
SMALL = pltpu.CompilerParams(vmem_limit_bytes=12 * 2**20)


def masked_dot(blocks, factors, rank):
    product = jnp.dot(blocks, factors, preferred_element_type=jnp.float32)
    lane = lax.broadcasted_iota(jnp.int32, product.shape, 1)
    return jnp.where(lane < rank, product, 0.0)


def pair(even, odd):
    lane = lax.broadcasted_iota(jnp.int32, even.shape, 1)
    front = jnp.where(lane < HALF, even, pltpu.roll(odd, HALF, 1))
    back = jnp.where(lane < HALF, pltpu.roll(even, HALF, 1), odd)
    return front.astype(BF16), back.astype(BF16)


def col_kernel(row_ref, me_ref, order_ref, rank_ref, z_ref, w_ref, *refs):
    out_refs, (z_buf, w_buf, first_buf, sems) = refs[: 2 + N_CORE], refs[2 + N_CORE : 6 + N_CORE]
    straight_buf, early_buf, *bufs = refs[6 + N_CORE : -1]
    out_sems = refs[-1]
    early, late = [], []
    for g in range(PB // STEP):
        part = pl.ds(g * STEP, STEP)
        early.append(pltpu.make_async_copy(z_ref.at[part], z_buf.at[part], sems.at[0, g]))
        early.append(pltpu.make_async_copy(w_ref.at[0, part], w_buf.at[0, part], sems.at[1, g]))
        late.append(pltpu.make_async_copy(w_ref.at[1, part], w_buf.at[1, part], sems.at[2, g]))
    for copy in early + late:
        copy.start()
    for g in range(PB // STEP):
        early[2 * g].wait()
        early[2 * g + 1].wait()
        blocks = range(g * STEP, (g + 1) * STEP)
        first = [masked_dot(z_buf[b], w_buf[0, b], rank_ref[0, b]) for b in blocks]
        for j in range(0, STEP, 2):
            front, back = pair(first[j], first[j + 1])
            first_buf[g * STEP + j] = front
            first_buf[g * STEP + j + 1] = back
    for copy in late:
        copy.wait()
    rows = CHUNKS[0]
    outs = []

    def send(buf, place, out_ref, start, count):
        copy = pltpu.make_async_copy(
            buf.at[pl.ds(place, count)], out_ref.at[pl.ds(start, count)], out_sems.at[len(outs)]
        )
        copy.start()
        outs.append(copy)

    for k in reversed(range(N_PLANE)):
        for m in range(N_Y):
            for e in range(N_CORE):
                for i in range(Q):
                    n = (m * N_CORE + e) * Q + i
                    place = (row_ref[0] ^ flip(k, m, e)) * Q + i
                    b = order_ref[place]
                    middle = masked_dot(first_buf[b], w_buf[1, b], rank_ref[1, b]).astype(BF16)
                    straight_buf[k * PIECE + near_place(row_ref, m, e) + i] = middle[:rows]
                    if k == EARLY:
                        early_buf[n] = middle[rows:]
                    else:
                        bufs[e][(k * N_Y + m) * Q + i] = middle[rows:]
        start = ((row_ref[0] // PLANE) ^ k) * PIECE
        send(straight_buf, k * PIECE, out_refs[0], start, PIECE)
        if k == EARLY:
            send(early_buf, 0, out_refs[1], 0, PIECE)
        else:
            for e in range(N_CORE):
                send(bufs[e], k * N_Y * Q, out_refs[2 + e], k * N_Y * Q, N_Y * Q)
    for copy in outs:
        copy.wait()


def near_place(row_ref, m, e):
    return ((row_ref[0] % PLANE) ^ (m * N_CORE + e)) * Q


def flip(k, m, e):
    return (k * N_Y + m) * N_CORE + e


def col_levels(row, me, order, ranks, right_sides, factors):
    straight, stepped = CHUNKS
    return pl.pallas_call(
        col_kernel,
        out_shape=[jax.ShapeDtypeStruct((PB, straight, BW), BF16)]
        + [jax.ShapeDtypeStruct((PIECE, stepped, BW), BF16)]
        + [jax.ShapeDtypeStruct((EARLY * N_Y * Q, stepped, BW), BF16)] * N_CORE,
        in_specs=[SMEM, SMEM, SMEM, SMEM, ANY, ANY],
        out_specs=[ANY] * (2 + N_CORE),
        scratch_shapes=[
            pltpu.VMEM((PB, R, BW), BF16),
            pltpu.VMEM((2, PB, BW, BW), BF16),
            pltpu.VMEM((PB, R, BW), BF16),
            pltpu.SemaphoreType.DMA((3, PB // STEP)),
            pltpu.VMEM((PB, straight, BW), BF16),
            pltpu.VMEM((PIECE, stepped, BW), BF16),
            pltpu.VMEM((EARLY * N_Y * Q, stepped, BW), BF16),
            pltpu.VMEM((EARLY * N_Y * Q, stepped, BW), BF16),
            pltpu.SemaphoreType.DMA((2 + EARLY * (1 + N_CORE),)),
        ],
        cost_estimate=pl.CostEstimate(
            flops=4 * PB * R * BW * BW, bytes_accessed=8 * 2**20, transcendentals=0
        ),
        name="col_levels",
    )(row, me, order, ranks, right_sides, factors)


def regroup_kernel(moves, n_in, *refs):
    for source, start, target, place in moves:
        refs[n_in + target][place : place + Q] = refs[source][start : start + Q]


def regroup(rows, moves, n_out, size, pieces, hint=0, after=()):
    return pl.pallas_call(
        functools.partial(regroup_kernel, moves, len(pieces) + len(after)),
        out_shape=[jax.ShapeDtypeStruct((size, rows, BW), BF16)] * n_out,
        in_specs=[VMEM] * len(pieces) + [ANY] * len(after),
        out_specs=[VMEM] * n_out,
        compiler_params=SMALL,
        cost_estimate=pl.CostEstimate(
            flops=hint, bytes_accessed=4 * n_out * size * rows * BW, transcendentals=0
        ),
        name="regroup",
    )(*pieces, *after)


def held(k, m, e):
    if e == 1:
        return 2, (k * N_Y + m) * Q
    if k == EARLY:
        return 1, m * N_CORE * Q
    return 0, (k * N_Y + m) * Q


def for_core():
    moves = []
    for k in range(N_PLANE):
        for m in range(N_Y):
            place = (k * N_Y + m) * Q
            if k == EARLY:
                moves.append((1, (m * N_CORE + 1) * Q, 0, place))
            else:
                moves.append((0, place, 0, place))
    return moves


def for_y():
    moves = []
    for m in range(1, N_Y):
        for e in range(N_CORE):
            for k in range(N_PLANE):
                moves.append((*held(k, m, e), m - 1, (e * N_PLANE + k) * Q))
    return moves


def for_planes():
    moves = []
    for k in range(N_PLANE):
        for m in range(N_Y):
            for e in range(N_CORE):
                place = (m * N_CORE + e) * Q
                if m == 0:
                    moves.append((*held(k, m, e), k, place))
                else:
                    moves.append((2 + m, (e * N_PLANE + k) * Q, k, place))
    return moves


def pick_kernel(me_ref, w_ref, far_ref, near_ref):
    for n, d in enumerate((2, 1, 3, 0)):
        for h in range(N_Z):
            base = (h * N_X + lax.rem(me_ref[0] + d, N_X)) * STEP
            out_ref, slot = (far_ref, h) if n == 0 else (near_ref, (n - 1) * N_Z + h)
            out_ref[slot * STEP : (slot + 1) * STEP] = w_ref[pl.ds(base, STEP)]


def pick_factors(me, factors):
    count = N_Z * STEP
    return pl.pallas_call(
        pick_kernel,
        out_shape=[
            jax.ShapeDtypeStruct((count, BW, BW), BF16),
            jax.ShapeDtypeStruct((PB - count, BW, BW), BF16),
        ],
        in_specs=[SMEM, VMEM],
        out_specs=[VMEM] * 2,
        compiler_params=SMALL,
        cost_estimate=pl.CostEstimate(
            flops=0, bytes_accessed=4 * PB * BW * BW, transcendentals=0
        ),
        name="pick_factors",
    )(me, factors)


def far_kernel(me_ref, rank_ref, z_ref, w_ref, after_ref, first_ref, second_ref):
    for h in range(N_Z):
        base = (h * N_X + lax.rem(me_ref[0] + 2, N_X)) * STEP
        for j in range(STEP):
            inner = masked_dot(z_ref[base + j], w_ref[h * STEP + j], rank_ref[base + j])
            out_ref = first_ref if j < SIDE else second_ref
            out_ref[h * SIDE + j % SIDE] = inner.astype(BF16)


def near_kernel(me_ref, rank_ref, z_ref, w_ref, after_ref, *out_refs):
    for n, d in enumerate((1, 3, 0)):
        for h in range(N_Z):
            base = (h * N_X + lax.rem(me_ref[0] + d, N_X)) * STEP
            for j in range(STEP):
                factors = w_ref[(n * N_Z + h) * STEP + j]
                inner = masked_dot(z_ref[base + j], factors, rank_ref[base + j])
                out_refs[n][h * STEP + j] = inner.astype(BF16)


def mid_part(kernel, name, rows, sizes, me, ranks, blocks, factors, after):
    count = factors.shape[0]
    return pl.pallas_call(
        kernel,
        out_shape=[jax.ShapeDtypeStruct((size, rows, BW), BF16) for size in sizes],
        in_specs=[SMEM, SMEM, VMEM, VMEM, ANY],
        out_specs=[VMEM] * len(sizes),
        compiler_params=SMALL,
        cost_estimate=pl.CostEstimate(
            flops=2 * count * rows * BW * BW + HINT_MID,
            bytes_accessed=count * (4 * rows + 2 * BW) * BW,
            transcendentals=0,
        ),
        name=name,
    )(me, ranks, blocks, factors, after)


def join_kernel(right_ref, left_ref, from_left_ref, from_right_ref, right_out, left_out):
    for h in range(N_Z):
        a, b = h * STEP, h * STEP + SIDE
        sides = slice(h * SIDE, (h + 1) * SIDE)
        first, second = slice(a, a + SIDE), slice(b, b + SIDE)
        right_out[first] = added(right_ref[first], from_left_ref[sides])
        right_out[second] = right_ref[second]
        left_out[first] = left_ref[first]
        left_out[second] = added(left_ref[second], from_right_ref[sides])


def added(a, b):
    return (a.astype(jnp.float32) + b.astype(jnp.float32)).astype(BF16)


def join_sides(rows, right, left, from_left, from_right):
    return pl.pallas_call(
        join_kernel,
        out_shape=[jax.ShapeDtypeStruct((N_Z * STEP, rows, BW), BF16)] * 2,
        in_specs=[VMEM] * 4,
        out_specs=[VMEM] * 2,
        compiler_params=SMALL,
        cost_estimate=pl.CostEstimate(
            flops=STEP * rows * BW + HINT_JOIN,
            bytes_accessed=12 * N_Z * STEP * rows * BW,
            transcendentals=0,
        ),
        name="join_sides",
    )(right, left, from_left, from_right)


def stepped_kernel(row_ref, me_ref, rank_ref, far_ref, near_ref, *refs):
    pieces, out_refs, block_buf = refs[:N_PLANE], refs[N_PLANE:-1], refs[-1]
    for k in range(N_PLANE):
        for m in range(N_Y):
            for e in range(N_CORE):
                b = (row_ref[0] ^ flip(k, m, e)) * Q
                at = (m * N_CORE + e) * Q
                block_buf[pl.ds(b, Q)] = pieces[k][at : at + Q]
    for n, d in enumerate((2, 1, 3, 0)):
        for h in range(N_Z):
            base = (h * N_X + lax.rem(me_ref[0] + d, N_X)) * STEP
            w_ref, slot = (far_ref, h) if n == 0 else (near_ref, (n - 1) * N_Z + h)
            for j in range(STEP):
                factors = w_ref[slot * STEP + j]
                inner = masked_dot(block_buf[base + j], factors, rank_ref[base + j])
                out_refs[d][h * STEP + j] = inner.astype(BF16)


def mid_stepped(rows, row, me, ranks, far_factors, near_factors, pieces):
    return pl.pallas_call(
        stepped_kernel,
        out_shape=[jax.ShapeDtypeStruct((N_Z * STEP, rows, BW), BF16)] * N_X,
        in_specs=[SMEM, SMEM, SMEM, VMEM, VMEM] + [VMEM] * N_PLANE,
        out_specs=[VMEM] * N_X,
        scratch_shapes=[pltpu.VMEM((PB, rows, BW), BF16)],
        compiler_params=SMALL,
        cost_estimate=pl.CostEstimate(
            flops=2 * PB * rows * BW * BW + HINT_STEPPED,
            bytes_accessed=PB * (4 * rows + 2 * BW) * BW,
            transcendentals=0,
        ),
        name="mid_stepped",
    )(row, me, ranks, far_factors, near_factors, *pieces)


def total_of(refs, half):
    total = refs[0][half].astype(jnp.float32)
    for ref in refs[1:]:
        total = total + ref[half].astype(jnp.float32)
    return total


def sum_kernel(me_ref, *refs):
    half = pl.ds((1 - lax.div(me_ref[0], N_X)) * STEP, STEP)
    refs[-1][...] = total_of(refs[:-1], half).astype(BF16)


def sum_other(rows, me, parts):
    return pl.pallas_call(
        sum_kernel,
        out_shape=jax.ShapeDtypeStruct((STEP, rows, BW), BF16),
        in_specs=[SMEM] + [VMEM] * len(parts),
        out_specs=VMEM,
        compiler_params=SMALL,
        cost_estimate=pl.CostEstimate(
            flops=4 * STEP * rows * BW, bytes_accessed=10 * STEP * rows * BW, transcendentals=0
        ),
        name="sum_other",
    )(me, *parts)


def row_kernel(me_ref, rank_ref, w_ref, *refs):
    out_ref, out_buf, sems = refs[-3:]
    base = me_ref[0] * OWN
    half = pl.ds(lax.div(me_ref[0], N_X) * STEP, STEP)
    totals = []
    for near, far in ((refs[:3], refs[3]), (refs[4 : 4 + N_X], refs[4 + N_X])):
        totals.append(total_of(near, half) + far[...].astype(jnp.float32))
    copies = []
    for j in range(0, OWN, 2):
        start = 0
        for total, rows in zip(totals, CHUNKS):
            for i, block in enumerate(pair(total[j], total[j + 1])):
                product = masked_dot(block, w_ref[base + j + i], rank_ref[base + j + i])
                out_buf[j + i, start : start + rows] = product.astype(BF16)
            start += rows
        two = pl.ds(j, 2)
        copies.append(pltpu.make_async_copy(out_buf.at[two], out_ref.at[two], sems.at[j // 2]))
        copies[-1].start()
    for copy in copies:
        copy.wait()


def row_level(me, ranks, factors, parts):
    return pl.pallas_call(
        row_kernel,
        out_shape=jax.ShapeDtypeStruct((OWN, R, BW), BF16),
        in_specs=[SMEM, SMEM, VMEM] + [VMEM] * len(parts),
        out_specs=ANY,
        scratch_shapes=[
            pltpu.VMEM((OWN, R, BW), BF16),
            pltpu.SemaphoreType.DMA((OWN // 2,)),
        ],
        compiler_params=SMALL,
        cost_estimate=pl.CostEstimate(
            flops=2 * OWN * R * BW * BW, bytes_accessed=2**20, transcendentals=0
        ),
        name="row_level",
    )(me, ranks, factors, *parts)


def around_x(value, d):
    pairs = [(z * N_X + x, z * N_X + (x + d) % N_X) for z in range(N_Z) for x in range(N_X)]
    return lax.ppermute(value, "col", pairs)


def across_z(value):
    half = N_X * N_Z // 2
    return lax.ppermute(value, "col", [(i, (i + half) % (2 * half)) for i in range(2 * half)])


def across_row(value, k, m, e):
    return lax.ppermute(
        value, "row", [(r, r ^ flip(k, m, e)) for r in range(N_PLANE * N_Y * N_CORE)]
    )


def shards(
    right_sides, col_factors, col_ranks, block_order, mid_factors, mid_ranks, row_factors, row_ranks
):
    me = lax.axis_index("col").astype(jnp.int32).reshape(1)
    row = lax.axis_index("row").astype(jnp.int32).reshape(1)
    ranks, factors = mid_ranks[0], mid_factors[0]
    straight_rows, stepped_rows = CHUNKS
    middle, early, same, other = col_levels(
        row, me, block_order[0], col_ranks, right_sides, col_factors
    )

    early = across_row(early, EARLY, 0, 0)
    regrouped = lax.all_to_all(middle, "row", split_axis=0, concat_axis=0, tiled=True)

    (other,) = regroup(
        stepped_rows, for_core(), 1, PB // N_CORE, [other, early], HINT_CORE
    )
    pieces = [same, early, across_row(other, 0, 0, 1)]
    lines = regroup(stepped_rows, for_y(), N_Y - 1, PIECE, pieces, HINT_Y)
    pieces += [across_row(line, 0, m + 1, 0) for m, line in enumerate(lines)]
    far_factors, near_factors = pick_factors(me, factors)
    planes = list(
        regroup(
            stepped_rows, for_planes(), N_PLANE, PIECE, pieces, HINT_PLANES, [far_factors]
        )
    )
    sent = planes[1]
    for k in range(1, EARLY):
        planes[k] = across_row(planes[k], k, 0, 0)

    first, second = mid_part(
        far_kernel, "mid_far", straight_rows, [STEP, STEP], me, ranks, regrouped, far_factors,
        sent,
    )
    right, left, own = mid_part(
        near_kernel, "mid_near", straight_rows, [N_Z * STEP] * 3, me, ranks, regrouped,
        near_factors, first,
    )
    from_left, from_right = around_x(first, 1), around_x(second, 3)
    right, left = join_sides(straight_rows, right, left, from_left, from_right)
    near = [own, around_x(right, 1), around_x(left, 3)]
    parts = near + [across_z(sum_other(straight_rows, me, near))]

    inner = mid_stepped(
        stepped_rows, row, me, ranks, far_factors, near_factors, planes
    )
    near = [inner[0]] + [around_x(inner[d], d) for d in (2, 1, 3)]
    parts += near + [across_z(sum_other(stepped_rows, me, near))]
    return row_level(me, row_ranks, row_factors, parts)


def solution(mesh):
    in_specs = (
        P(("col", "row"), None, None),
        P(None, ("col", "row"), None, None),
        P(None, ("col", "row")),
        P(("col", "row"), None),
        P("col", "row", None, None),
        P("col", "row"),
        P("row", None, None),
        P("row"),
    )
    out_specs = P(("row", "col"), None, None)
    return jax.shard_map(shards, mesh=mesh, in_specs=in_specs, out_specs=out_specs, check_vma=False)
```
